512 devices in a mesh: fsdp: 128 (over z, y, core), dp: 4 (over x).
Axes of the slice: x: 4, y: 8, z: 8, core: 2. Of those that a mesh axis runs over, the one named last changes fastest.
Arguments:
- tokens: bfloat16 [4, 512, 6144], P('dp', 'fsdp')
- act_cot: bfloat16 [4, 512, 12288], P('dp', None, 'fsdp')
- old_slots: bfloat16 [113255424], P('fsdp'), as said below
- offsets: int32 [129], replicated, may hold values from 0 to 75503616, as said below
Outputs:
- grad_shards: float32 [75503616], P('fsdp')
The draws below stay inside these ranges and needn't reach their ends.
Inputs may be any that keep to these rules, and one draw needn't show every extreme that they name: offsets[0] is 0 and offsets[128] is 75503616; every offsets[i] lies within 147468 of i * 589872; one old range is exactly 884808 long in every draw. `old_slots`: slots past an owner's range hold arbitrary values.
All inputs are finite; a program needn't handle non-finite values.
Results may differ from the reference program's by a relative error of at most 0.0032.
The reference program's roundings to bfloat16 on the way (of `params`, `scaled` and `pre_grad`) count: a program that leaves them out, or rounds other values in their place, can miss the bound.
Values may be sent and summed in bfloat16 or wider, within the bound.
A program may use at most 64 MiB of HBM per device.

```python
import math
import jax
import jax.numpy as jnp
from jax import lax

D = 6144
HID = 12288
TOKENS = 2048
REPLICA_ROWS = 512
HID_DEV = 96
GAIN_DEV = 48
FLAT = 75503616
SHARD = 589872
QUARTER = 147468
MAXLEN = 884808
N_FSDP = 128
N_DP = 4


def owner_offsets(key):
    key_shift, key_busy = jax.random.split(key)
    rank_ids = jnp.arange(N_FSDP + 1, dtype=jnp.int32)
    shifts = jax.random.randint(key_shift, (N_FSDP + 1,), -QUARTER, QUARTER + 1)
    busiest = jax.random.randint(key_busy, (), 1, N_FSDP - 1)
    shifts = jnp.where(rank_ids == busiest, -QUARTER, shifts)
    shifts = jnp.where(rank_ids == busiest + 1, QUARTER, shifts)
    shifts = jnp.where((rank_ids == 0) | (rank_ids == N_FSDP), 0, shifts)
    return (rank_ids * SHARD + shifts).astype(jnp.int32)


def draw_offsets(key, part):
    return owner_offsets(key)


def draw_old_slots(key, part):
    bounds = owner_offsets(key)
    key = jax.random.fold_in(key, 9)
    key_unit, key_gain, key_fill = jax.random.split(key, 3)
    unit_draw = jax.random.normal(key_unit, (FLAT,), jnp.float32)
    positions = jnp.arange(FLAT, dtype=jnp.int32)
    within = positions % SHARD
    gain_draw = 0.5 + jax.random.uniform(key_gain, (FLAT,), jnp.float32)
    params = jnp.where(within < HID_DEV * D, unit_draw * D ** (-0.5), gain_draw)
    filler = jax.random.normal(key_fill, (N_FSDP, MAXLEN), jnp.float32)
    slot_ids = jnp.arange(MAXLEN, dtype=jnp.int32)
    lengths = bounds[1:] - bounds[:-1]
    target = bounds[:-1, None] + slot_ids[None, :]
    is_valid = slot_ids[None, :] < lengths[:, None]
    values = jnp.where(is_valid, params[jnp.clip(target, 0, FLAT - 1)], filler)
    return values.reshape(-1).astype(jnp.bfloat16)


def draw_tokens(key, part):
    key = jax.random.fold_in(key, 11)
    key_base, key_cols, key_rows = jax.random.split(key, 3)
    shape = (N_DP, REPLICA_ROWS, D)
    base_draw = jax.random.normal(key_base, shape, jnp.float32)
    col_scale = jnp.exp(jax.random.uniform(key_cols, (1, 1, D), jnp.float32) * math.log(10.0))
    row_scale = jnp.exp(jax.random.uniform(key_rows, (N_DP, REPLICA_ROWS, 1), jnp.float32) * math.log(10.0))
    return (base_draw * col_scale * row_scale).astype(jnp.bfloat16)


def draw_act_cot(key, part):
    key = jax.random.fold_in(key, 13)
    key_base, key_cols = jax.random.split(key, 2)
    shape = (N_DP, REPLICA_ROWS, HID)
    base_draw = jax.random.normal(key_base, shape, jnp.float32)
    rising = jnp.exp(math.log(3.0) * jnp.arange(HID, dtype=jnp.float32) / HID)
    rough = jnp.exp(jax.random.uniform(key_cols, (HID,), jnp.float32) * math.log(2.0))
    return (base_draw * (rising * rough)[None, None, :] * TOKENS ** (-0.5)).astype(jnp.bfloat16)


def setup_inputs(seed: int = 0) -> dict:
    arg_keys = jax.random.split(jax.random.key(seed), 5)
    return {
        "tokens": draw_tokens(jax.random.fold_in(arg_keys[4], 71), 0),
        "act_cot": draw_act_cot(jax.random.fold_in(arg_keys[4], 71), 0),
        "old_slots": draw_old_slots(jax.random.fold_in(arg_keys[4], 71), 0),
        "offsets": draw_offsets(jax.random.fold_in(arg_keys[4], 71), 0),
    }


EPSILON = 1e-06

def place_slots(old_slots, offsets):
    padded = old_slots.reshape(N_FSDP, MAXLEN)
    slot_ids = jnp.arange(MAXLEN, dtype=jnp.int32)
    lengths = (offsets[1:] - offsets[:-1]).astype(jnp.int32)
    target = offsets[:-1, None].astype(jnp.int32) + slot_ids[None, :]
    target = jnp.where(slot_ids[None, :] < lengths[:, None], target, FLAT).astype(jnp.int32)
    empty = jnp.zeros((FLAT,), jnp.bfloat16)
    return empty.at[target.reshape(-1)].set(padded.reshape(-1), mode='drop')

def reference(tokens, act_cot, old_slots, offsets):
    params = place_slots(old_slots, offsets).reshape(N_FSDP, SHARD)
    w_in = params[:, :HID_DEV * D].reshape(HID, D)
    norm_gain = params[:, HID_DEV * D:].reshape(D)
    as_float = tokens.reshape(TOKENS, D).astype(jnp.float32)
    row_mean = lax.optimization_barrier(jnp.mean(as_float, axis=-1, keepdims=True))
    centered = as_float - row_mean
    variance = lax.optimization_barrier(jnp.mean(centered * centered, axis=-1, keepdims=True))
    normed = centered * lax.rsqrt(variance + EPSILON)
    scaled = (normed * norm_gain.astype(jnp.float32)).astype(jnp.bfloat16)
    pre_act = lax.dot_general(scaled, w_in, (((1,), (1,)), ((), ())), preferred_element_type=jnp.float32)
    _, gelu_back = jax.vjp(jax.nn.gelu, pre_act)
    cot_float = act_cot.reshape(TOKENS, HID).astype(jnp.float32)
    pre_grad = gelu_back(cot_float)[0].astype(jnp.bfloat16)
    grad_in = lax.dot_general(pre_grad, scaled, (((0,), (0,)), ((), ())), preferred_element_type=jnp.float32)
    moment = lax.dot_general(pre_grad.astype(jnp.float32), normed, (((0,), (0,)), ((), ())), precision=lax.Precision.HIGHEST, preferred_element_type=jnp.float32)
    gain_grad = lax.optimization_barrier(jnp.sum(w_in.astype(jnp.float32) * moment, axis=0))
    joined = jnp.concatenate([grad_in.reshape(N_FSDP, HID_DEV * D), gain_grad.reshape(N_FSDP, GAIN_DEV)], axis=1)
    return joined.reshape(-1)
```

```python
import jax
import jax.numpy as jnp
import numpy as np
from jax import lax
from jax.experimental import pallas as pl
from jax.experimental.pallas import tpu as pltpu
from jax.sharding import PartitionSpec as P

D = 6144
HID_DEV = 96
SHARD = 589872
EPSILON = 1e-06
LINES = 6928
FRONT = 2704
BACK = 384
BLOCK = 768
LANES = 128
A_ROWS = 112
C_ROWS = 208
F32 = jnp.float32
BF16 = jnp.bfloat16


def lane_iota(rows):
    return lax.broadcasted_iota(jnp.int32, (rows, LANES), 1)


def three_terms(value):
    high = value.astype(BF16).astype(F32)
    rest = value - high
    mid = rest.astype(BF16).astype(F32)
    return high, mid, rest - mid


def prepare_kernel(tok_ref, slots_ref, off_ref, msg_ref, own_ref, right_ref, left_ref, wide, lines, packed):
    x = lax.axis_index("dp")
    j = lax.axis_index("fsdp")
    start = off_ref[j]
    length = off_ref[j + 1] - start
    shift_own = j * SHARD - start
    shift_right = shift_own + SHARD
    shift_left = shift_own - SHARD

    def widen(i, carry):
        rows = pl.ds(pl.multiple_of(i * 16, 16), 16)
        wide[pl.ds(pl.multiple_of(FRONT + i * 16, 16), 16), :] = slots_ref[rows, :].astype(F32)
        return carry

    lax.fori_loop(0, LINES // 16, widen, 0, unroll=8)

    def extract(first, shift, rows):
        turn = shift & (LANES - 1)
        at = FRONT + first + lax.shift_right_arithmetic(shift, 7)
        here = wide[pl.ds(at, rows), :]
        after = wide[pl.ds(at + 1, rows), :]
        back = (LANES - turn) & (LANES - 1)
        lane = lane_iota(rows)
        line = lax.broadcasted_iota(jnp.int32, (rows, LANES), 0)
        moved = jnp.where(lane < LANES - turn, pltpu.roll(here, back, 1), pltpu.roll(after, back, 1))
        slot = (first + line) * LANES + lane + shift
        return jnp.where((slot >= 0) & (slot < length), moved, 0.0)

    def piece(out_ref, first_row, rows, shift):
        def one(h, carry):
            got = extract((first_row + h) * 48 + 12 * x, shift, 16)
            lines[pl.ds(pl.multiple_of(h * 16, 16), 16), :] = got
            return carry

        lax.fori_loop(0, rows, one, 0, unroll=4)
        for k in range(12):
            col = lines[pl.ds(k, rows, stride=16), :]
            out_ref[k // 6, :, (k % 6) * LANES : (k % 6 + 1) * LANES] = col.astype(BF16)

    piece(own_ref, 0, 96, shift_own)
    piece(right_ref, 0, 32, shift_right)
    piece(left_ref, 64, 32, shift_left)

    lane8 = lane_iota(8)
    gain_own = extract(0, shift_own + HID_DEV * D - 16, 8)
    gain_left = extract(0, shift_left + HID_DEV * D - 64, 8)
    gains = jnp.where(
        (lane8 >= 16) & (lane8 < 64), gain_own, jnp.where((lane8 >= 64) & (lane8 < 112), gain_left, 0.0)
    )[0:1]

    tok = tok_ref[0].astype(F32)
    mean = jnp.mean(tok, axis=-1, keepdims=True)
    centered = tok - mean
    variance = jnp.mean(centered * centered, axis=-1, keepdims=True)
    scale = lax.rsqrt(variance + EPSILON)
    lane4 = lane_iota(4)
    extra = jnp.where((lane4 >= 16) & (lane4 < 112), jnp.broadcast_to(gains, (4, LANES)), 0.0)
    for n, term in enumerate(three_terms(mean) + three_terms(scale)):
        extra = jnp.where((lane4 == n) | (lane4 == n + 8), term, extra)
    for b in range(8):
        for k in range(6):
            col = (6 * b + k) * LANES
            packed[32 * b + 4 * k : 32 * b + 4 * k + 4, :] = tok[:, col : col + LANES]
        packed[32 * b + 24 : 32 * b + 28, :] = extra
        packed[32 * b + 28 : 32 * b + 32, :] = jnp.zeros((4, LANES), F32)
    for b in range(8):
        msg_ref[b] = packed[32 * b : 32 * b + 32, :].astype(BF16)


def gelu_slope(v):
    root = 0.7978845608028654
    t = jnp.tanh(root * (v + 0.044715 * (v * v * v)))
    return 0.5 * (1.0 + t) + 0.5 * v * (1.0 - t * t) * (root * (1.0 + 3 * 0.044715 * (v * v)))


def main_kernel(
    msg_ref, own_ref, right_ref, left_ref, cot_ref, pick_ref, mask_ref, out_ref,
    mail, edge_right, edge_left, weight, gath, norm, scaled, part, part_in, sums, sums_in,
    grads, result, spill, block_out, gain_rows, gain_mine, gain_z, gain_y, gain_out,
    mail_s, mail_r, edge_s, edge_r, core_s, core_r, one_s, one_r, two_s, two_r,
    sum_s, sum_r, pg_s, pg_r, res_s, res_r, gz_s, gz_r, gy_s, gy_r, gf_s, gf_r,
):
    x = lax.axis_index("dp")
    f = lax.axis_index("fsdp")
    c = f % 2
    y = (f // 2) % 8
    z = f // 16
    g = 2 * x + c
    other = 1 - c
    su = 2 + 14 * c
    sv = 16 - 14 * c
    pu = y + c * (z - y)
    pv = z + c * (y - z)
    sends = []

    def at(xx, ff):
        return {"dp": xx, "fsdp": ff}

    def mate(gg):
        return at(gg // 2, f - c + gg % 2)

    def dev_u(d):
        return at(x, ((pu + d + 8) % 8) * su + pv * sv + c)

    def dev_v(d):
        return at(x, pu * su + ((pv + d + 8) % 8) * sv + c)

    def dev_y(d):
        return at(x, z * 16 + ((y + d) % 8) * 2 + c)

    def dev_z(d):
        return at(x, ((z + d) % 8) * 16 + y * 2 + c)

    def dev_x(d):
        return at((x + d + 4) % 4, f)

    core = at(x, f - c + other)
    right = at(x, (f + 1) % 128)
    left = at(x, (f + 127) % 128)

    def copy(src, dst, ssem, rsem, dev):
        return pltpu.make_async_remote_copy(
            src_ref=src, dst_ref=dst, send_sem=ssem, recv_sem=rsem,
            device_id=dev, device_id_type=pl.DeviceIdType.MESH,
        )

    def send(src, dst, ssem, rsem, dev):
        one = copy(src, dst, ssem, rsem, dev)
        one.start()
        sends.append(one)

    def arrive(dst, ssem, rsem):
        copy(dst, dst, ssem, rsem, core).wait_recv()

    barrier = pltpu.get_barrier_semaphore()
    peers = [mate((g + r) % 8) for r in range(1, 8)]
    peers += [dev_y(r) for r in range(1, 8)] + [dev_z(r) for r in range(1, 8)] + [right, left]
    for dev in peers:
        pl.semaphore_signal(barrier, inc=1, device_id=dev, device_id_type=pl.DeviceIdType.MESH)
    pl.semaphore_wait(barrier, len(peers))

    for r in range(1, 8):
        gg = (g + r) % 8
        send(msg_ref.at[gg], mail.at[g], mail_s.at[r - 1], mail_r.at[r - 1], mate(gg))
    send(right_ref, edge_right, edge_s.at[0], edge_r.at[0], right)
    send(left_ref, edge_left, edge_s.at[1], edge_r.at[1], left)
    mail[pl.ds(g, 1)] = msg_ref[pl.ds(g, 1)]
    for r in range(1, 8):
        arrive(mail.at[(g - r + 8) % 8], mail_s.at[r - 1], mail_r.at[r - 1])

    letters = mail[...].reshape(256, LANES)
    out_row = lax.broadcasted_iota(jnp.int32, (C_ROWS, 256), 0)
    in_row = lax.broadcasted_iota(jnp.int32, (C_ROWS, 256), 1)
    token = out_row & 31
    want = 32 * (token >> 2) + 4 * (out_row >> 5) + (token & 3)
    chunk = jnp.dot((want == in_row).astype(BF16), letters, preferred_element_type=F32)
    out_row = lax.broadcasted_iota(jnp.int32, (16, 256), 0) + 16
    in_row = lax.broadcasted_iota(jnp.int32, (16, 256), 1)
    want = 32 * (out_row >> 2) + 24 + (out_row & 3)
    late = jnp.dot((want == in_row).astype(BF16), letters, preferred_element_type=F32)
    lane = lane_iota(16)
    extra = jnp.where((lane >= 8) & (lane < 16), late, chunk[192:208])
    gath[pu, pv, 0:192, :] = chunk[0:192].astype(BF16)
    gath[pu, pv, 192:208, :] = extra.astype(BF16)

    def first_a(i):
        return gath.at[i, pv, 0:A_ROWS]

    def first_b(i):
        return gath.at[pu, i, A_ROWS:C_ROWS]

    def second_a(h, i):
        return gath.at[4 * h : 4 * h + 4, i, 0:A_ROWS]

    def second_b(h, i):
        return gath.at[i, 4 * h : 4 * h + 4, A_ROWS:C_ROWS]

    streams = ((first_a, pu, dev_u, 1), (first_b, pv, dev_v, -1))
    for s in range(1, 5):
        for n, (slot, p, dev, full) in enumerate(streams):
            for m, d in enumerate((1, -1)):
                if s < 4 or d == full:
                    src = slot((p - d * (s - 1) + 8) % 8)
                    send(src, src, one_s.at[n, m, s - 1], one_r.at[n, m, s - 1], dev(d))
        for n, (slot, p, dev, full) in enumerate(streams):
            for m, d in enumerate((1, -1)):
                if s < 4 or d == full:
                    arrive(slot((p - d * s + 8) % 8), one_s.at[n, m, s - 1], one_r.at[n, m, s - 1])

    streams = ((second_a, pv, dev_v), (second_b, pu, dev_u))
    for s in range(1, 6):
        for h in range(2):
            for n, (slot, p, dev) in enumerate(streams):
                for m, d in enumerate((1, -1)):
                    if 1 < s and (s < 5 or h == m):
                        arrive(slot(h, (p - d * (s - 1) + 8) % 8), two_s.at[n, m, h, s - 2], two_r.at[n, m, h, s - 2])
                    if s < 4 or (s == 4 and h == m):
                        src = slot(h, (p - d * (s - 1) + 8) % 8)
                        send(src, src, two_s.at[n, m, h, s - 1], two_r.at[n, m, h, s - 1], dev(d))

        if s == 1:
            arrive(edge_right, edge_s.at[0], edge_r.at[0])
            arrive(edge_left, edge_s.at[1], edge_r.at[1])
            for half in range(2):
                spill[half, 0:32, :] = own_ref[half, 0:32, :] + edge_right[half]
                spill[half, 32:64, :] = own_ref[half, 32:64, :]
                spill[half, 64:96, :] = own_ref[half, 64:96, :] + edge_left[half]
            send(spill.at[other], weight.at[c], core_s.at[0], core_r.at[0], core)
            weight[pl.ds(c, 1)] = spill[pl.ds(c, 1)]
    arrive(weight.at[other], core_s.at[0], core_r.at[0])

    def chip(yy, zz):
        return yy + c * (zz - yy), zz + c * (yy - zz)

    for yy in range(9):
        uu, vv = chip(yy % 8, (g + yy // 8) % 8)
        rows = gath[uu, vv, 192:208, :].astype(F32)
        if yy < 8:
            gain_rows[2 * yy : 2 * yy + 1, :] = rows[0:1]
            gain_rows[2 * yy + 1 : 2 * yy + 2, :] = rows[4:5]
            gain_rows[16 + 2 * yy : 17 + 2 * yy, :] = rows[4:5]
        if yy > 0:
            gain_rows[15 + 2 * yy : 16 + 2 * yy, :] = rows[0:1]
    spread = jnp.dot(gain_rows[0:16, :].astype(BF16), pick_ref[0], preferred_element_type=F32)
    spread += jnp.dot(gain_rows[16:32, :].astype(BF16), pick_ref[1], preferred_element_type=F32)
    gain = jnp.sum(spread * mask_ref[...], axis=0, keepdims=True)

    def normalize(i, carry):
        zz = i // 4
        pair = i % 4
        data = []
        for side in range(2):
            uu, vv = chip(2 * pair + side, zz)
            rows = gath[uu, vv, 192:208, :].astype(F32)
            cols = []
            for base in (0, 3):
                early = (rows[:, base : base + 1] + rows[:, base + 1 : base + 2]) + rows[:, base + 2 : base + 3]
                late = (rows[:, base + 8 : base + 9] + rows[:, base + 9 : base + 10]) + rows[:, base + 10 : base + 11]
                cols.append((early[0:8], early[8:16], late[0:8], late[8:16]))
            data.append((uu, vv, cols))
        for k in range(6):
            gain_k = gain[:, k * LANES : (k + 1) * LANES]
            tiles = [gath[uu, vv, 32 * k : 32 * k + 32, :].astype(F32) for uu, vv, _ in data]
            for xx in range(4):
                both = jnp.concatenate(
                    [
                        (tiles[side][8 * xx : 8 * xx + 8] - data[side][2][0][xx]) * data[side][2][1][xx]
                        for side in range(2)
                    ],
                    axis=0,
                )
                rows = pl.ds(pl.multiple_of(512 * xx + 16 * i, 16), 16)
                norm[rows, k * LANES : (k + 1) * LANES] = both
                scaled[rows, k * LANES : (k + 1) * LANES] = (both * gain_k).astype(BF16)
        return carry

    lax.fori_loop(0, 32, normalize, 0)

    block = weight[...].reshape(192, BLOCK)
    for xx in range(4):
        for half in range(2):
            at_row = 512 * xx + 256 * half
            got = lax.dot_general(
                block, scaled[at_row : at_row + 256, :], (((1,), (1,)), ((), ())), preferred_element_type=F32
            )
            part[0, xx, :, 256 * half : 256 * half + 256] = got[0:96]
            part[1, xx, :, 256 * half : 256 * half + 256] = got[96:192]
    send(part.at[other], part_in, core_s.at[1], core_r.at[1], core)
    arrive(part_in, core_s.at[1], core_r.at[1])
    sums[...] = part[pl.ds(c, 1)][0] + part_in[...]
    for r in range(1, 4):
        send(sums.at[(x + r) % 4], sums_in.at[r - 1], sum_s.at[r - 1], sum_r.at[r - 1], dev_x(r))
    for r in range(1, 4):
        arrive(sums_in.at[r - 1], sum_s.at[r - 1], sum_r.at[r - 1])
    pre_act = (sums[pl.ds(x, 1)][0] + sums_in[0]) + (sums_in[1] + sums_in[2])
    pre_grad = (cot_ref[...].astype(F32) * gelu_slope(pre_act)).astype(BF16)

    mine = pl.ds(pl.multiple_of(96 * c, 32), 96)
    theirs = pl.ds(pl.multiple_of(96 * other, 32), 96)
    grads[pl.ds(x, 1), mine, :] = pre_grad[None]
    for r in range(1, 4):
        send(grads.at[x, mine], grads.at[x, mine], pg_s.at[r - 1], pg_r.at[r - 1], dev_x(r))
    for r in range(1, 4):
        arrive(grads.at[(x - r + 4) % 4, mine], pg_s.at[r - 1], pg_r.at[r - 1])
    send(grads.at[:, mine], grads.at[:, mine], core_s.at[2], core_r.at[2], core)
    arrive(grads.at[:, theirs], core_s.at[2], core_r.at[2])

    total = jnp.zeros((192, BLOCK), F32)
    for xx in range(4):
        total += jnp.dot(grads[xx], scaled[512 * xx : 512 * xx + 512, :], preferred_element_type=F32)
    rounded = total.astype(BF16)
    block_out[0] = rounded[0:96]
    block_out[1] = rounded[96:192]
    send(block_out.at[other], result.at[x, c], core_s.at[3], core_r.at[3], core)
    result[pl.ds(x, 1), pl.ds(c, 1)] = block_out[pl.ds(c, 1)][None]
    for m, d in enumerate((1, -1)):
        send(result.at[x, c], result.at[x, c], res_s.at[m, 0], res_r.at[m, 0], dev_x(d))
    arrive(result.at[x, other], core_s.at[3], core_r.at[3])
    for m, d in enumerate((1, -1)):
        send(result.at[x, other], result.at[x, other], res_s.at[m, 1], res_r.at[m, 1], dev_x(d))

    gain_sum = jnp.zeros((1, BLOCK), F32)
    for xx in range(4):
        for half in range(2):
            back = lax.dot_general(
                grads[xx, :, 256 * half : 256 * half + 256], block, (((0,), (0,)), ((), ())),
                preferred_element_type=F32,
            )
            at_row = 512 * xx + 256 * half
            gain_sum += jnp.sum(back * norm[at_row : at_row + 256, :], axis=0, keepdims=True)
    for k in range(6):
        gain_mine[k : k + 1, :] = gain_sum[:, k * LANES : (k + 1) * LANES]
    gain_mine[6:8, :] = jnp.zeros((2, LANES), F32)
    apart = (z - g + 8) % 8

    arrive(result.at[(x + 3) % 4, c], res_s.at[0, 0], res_r.at[0, 0])
    arrive(result.at[(x + 1) % 4, c], res_s.at[1, 0], res_r.at[1, 0])
    arrive(result.at[(x + 3) % 4, other], res_s.at[0, 1], res_r.at[0, 1])
    send(result.at[(x + 3) % 4, 0], result.at[(x + 3) % 4, 0], res_s.at[0, 2], res_r.at[0, 2], dev_x(1))
    arrive(result.at[(x + 1) % 4, other], res_s.at[1, 1], res_r.at[1, 1])
    send(result.at[(x + 1) % 4, 1], result.at[(x + 1) % 4, 1], res_s.at[1, 2], res_r.at[1, 2], dev_x(-1))

    @pl.when(apart != 0)
    def _():
        to_z = copy(
            gain_mine, gain_z.at[apart - 1], gz_s, gz_r.at[apart - 1], at(x, g * 16 + y * 2 + c)
        )
        to_z.start()
        to_z.wait_send()

    @pl.when(apart == 0)
    def _():
        sum_z = gain_mine[...]
        for r in range(7):
            arrive(gain_z.at[r], gz_s, gz_r.at[r])
            sum_z += gain_z[r]
        gain_y[7] = sum_z
        outs = [
            copy(gain_y.at[7], gain_y.at[r - 1], gy_s.at[r - 1], gy_r.at[r - 1], dev_y(r)) for r in range(1, 8)
        ]
        for one in outs:
            one.start()
        for r in range(7):
            arrive(gain_y.at[r], gy_s.at[r], gy_r.at[r])
            sum_z += gain_y[r]
        gain_out[...] = sum_z
        for one in outs:
            one.wait_send()
        outs = [copy(gain_out, gain_out, gf_s.at[r - 1], gf_r, mate((g + r) % 8)) for r in range(1, 8)]
        for one in outs:
            one.start()
        for one in outs:
            one.wait_send()

    @pl.when(apart != 0)
    def _():
        arrive(gain_out, gf_s.at[0], gf_r)

    first = 48 * (2 * y + c)
    turn = first % LANES
    line = first // LANES
    here = jnp.broadcast_to(gain_out[pl.ds(line, 1), :], (8, LANES))
    after = jnp.broadcast_to(gain_out[pl.ds(line + 1, 1), :], (8, LANES))
    back = (LANES - turn) % LANES
    moved = jnp.where(lane_iota(8) < LANES - turn, pltpu.roll(here, back, 1), pltpu.roll(after, back, 1))
    out_ref[4608:4616, :] = moved

    def spell(xx, half):
        for k in range(6):
            col = result[xx, half, :, k * LANES : (k + 1) * LANES].astype(F32)
            out_ref[pl.ds(12 * xx + 6 * half + k, 96, stride=48), :] = col

    arrive(result.at[(x + 2) % 4, 0], res_s.at[0, 2], res_r.at[0, 2])
    arrive(result.at[(x + 2) % 4, 1], res_s.at[1, 2], res_r.at[1, 2])
    for xx in range(4):
        for half in range(2):
            spell(xx, half)
    for one in sends:
        one.wait_send()


def body(tokens, act_cot, old_slots, offsets):
    vmem = pl.BlockSpec(memory_space=pltpu.VMEM)
    smem = pl.BlockSpec(memory_space=pltpu.SMEM)
    dma = pltpu.SemaphoreType.DMA
    slots = jnp.pad(old_slots, (0, LINES * LANES - old_slots.shape[0])).reshape(LINES, LANES)
    msg, own, right, left = pl.pallas_call(
        prepare_kernel,
        out_shape=[
            jax.ShapeDtypeStruct((8, 32, LANES), BF16),
            jax.ShapeDtypeStruct((2, 96, BLOCK), BF16),
            jax.ShapeDtypeStruct((2, 32, BLOCK), BF16),
            jax.ShapeDtypeStruct((2, 32, BLOCK), BF16),
        ],
        in_specs=[vmem, vmem, smem],
        out_specs=[vmem] * 4,
        scratch_shapes=[
            pltpu.VMEM((FRONT + LINES + BACK, LANES), F32),
            pltpu.VMEM((96 * 16, LANES), F32),
            pltpu.VMEM((256, LANES), F32),
        ],
        compiler_params=pltpu.CompilerParams(vmem_limit_bytes=24 * 2**20),
    )(tokens, slots, offsets)

    n = np.arange(BLOCK)
    lanes = np.arange(LANES)[:, None]
    pick = jnp.asarray(np.stack([lanes == 16 + n % 48, lanes == 64 + n % 48]).astype(np.float32), BF16)
    mask = jnp.asarray((np.arange(16)[:, None] == n // 48).astype(np.float32))
    out = pl.pallas_call(
        main_kernel,
        out_shape=jax.ShapeDtypeStruct((4616, LANES), F32),
        in_specs=[vmem] * 7,
        out_specs=vmem,
        scratch_shapes=[
            pltpu.VMEM((8, 32, LANES), BF16),
            pltpu.VMEM((2, 32, BLOCK), BF16),
            pltpu.VMEM((2, 32, BLOCK), BF16),
            pltpu.VMEM((2, 96, BLOCK), BF16),
            pltpu.VMEM((8, 8, C_ROWS, LANES), BF16),
            pltpu.VMEM((2048, BLOCK), F32),
            pltpu.VMEM((2048, BLOCK), BF16),
            pltpu.VMEM((2, 4, 96, 512), F32),
            pltpu.VMEM((4, 96, 512), F32),
            pltpu.VMEM((4, 96, 512), F32),
            pltpu.VMEM((3, 96, 512), F32),
            pltpu.VMEM((4, 192, 512), BF16),
            pltpu.VMEM((4, 2, 96, BLOCK), BF16),
            pltpu.VMEM((2, 96, BLOCK), BF16),
            pltpu.VMEM((2, 96, BLOCK), BF16),
            pltpu.VMEM((32, LANES), F32),
            pltpu.VMEM((8, LANES), F32),
            pltpu.VMEM((7, 8, LANES), F32),
            pltpu.VMEM((8, 8, LANES), F32),
            pltpu.VMEM((8, LANES), F32),
            dma((7,)), dma((7,)),
            dma((2,)), dma((2,)),
            dma((4,)), dma((4,)),
            dma((2, 2, 4)), dma((2, 2, 4)),
            dma((2, 2, 2, 4)), dma((2, 2, 2, 4)),
            dma((3,)), dma((3,)),
            dma((3,)), dma((3,)),
            dma((2, 3)), dma((2, 3)),
            dma, dma((7,)),
            dma((7,)), dma((7,)),
            dma((7,)), dma,
        ],
        compiler_params=pltpu.CompilerParams(
            collective_id=0, has_side_effects=True, vmem_limit_bytes=48 * 2**20
        ),
    )(msg, own, right, left, act_cot[0].T, pick, mask)
    return out.reshape(-1)[:SHARD]


def solution(mesh):
    placed = (P("dp", "fsdp", None), P("dp", None, "fsdp"), P("fsdp"), P())
    return jax.shard_map(body, mesh=mesh, in_specs=placed, out_specs=P("fsdp"), check_vma=False)
```

```python
import jax
import jax.numpy as jnp
import numpy as np
from jax import lax
from jax.experimental import pallas as pl
from jax.experimental.pallas import tpu as pltpu
from jax.sharding import PartitionSpec as P

D = 6144
HID_DEV = 96
SHARD = 589872
EPSILON = 1e-06
LINES = 6928
FRONT = 2704
BACK = 384
BLOCK = 768
LANES = 128
A_ROWS = 112
B_ROWS = 96
F32 = jnp.float32
BF16 = jnp.bfloat16
AWAY = (0, 1, -1, 2, -2, 3, -3, 4)
SLOT = {d: n for n, d in enumerate(AWAY)}
SLOT[-4] = SLOT[4]
SETS = ((0, 128), (128, 256), (384, 128))


def chips_in_order():
    near = [(a, b) for b in range(4) for a in range(4)]
    mid = [(4 + e % 3, e // 3) for e in range(12)] + [(e % 7, 4 + e // 7) for e in range(20)]
    far = [(e, 7) for e in range(8)] + [(7 - e // 15, e - 8 - e // 15) for e in range(8, 16)]
    return near + mid + far


def lane_iota(rows):
    return lax.broadcasted_iota(jnp.int32, (rows, LANES), 1)


def three_terms(value):
    high = value.astype(BF16).astype(F32)
    rest = value - high
    mid = rest.astype(BF16).astype(F32)
    return high, mid, rest - mid


def gelu_slope(v):
    root = 0.7978845608028654
    t = jnp.tanh(root * (v + 0.044715 * (v * v * v)))
    return 0.5 * (1.0 + t) + 0.5 * v * (1.0 - t * t) * (root * (1.0 + 3 * 0.044715 * (v * v)))


def main_kernel(
    tok_ref, slots_ref, off_ref, cot_ref, away_ref, pick_ref, mask_ref, out_ref,
    wide, lines, packed, letters, mail, own, right_out, left_out, edge_right, edge_left,
    spill, weight, gath_a, gath_b, cot, norm, scaled,
    part_1, part_2, part_3, part_in_1, part_in_2, part_in_3,
    sums_1, sums_2, sums_3, sums_in_1, sums_in_2, sums_in_3, grads_1, grads_2, grads_3,
    acc, result, block_out, gain_own, gain_tiles, gain_rows, gain_mine, gain_z, gain_y, gain_out,
    mail_s, mail_r, edge_s, edge_r, core_s, core_r, one_s, one_r, two_s, two_r,
    half_s, half_r, sum_s, sum_r, pg_s, pg_r, pgc_s, pgc_r, res_s, res_r,
    gty_s, gty_r, gtz_s, gtz_r, gz_s, gz_r, gy_s, gy_r, gf_s, gf_r,
):
    part = (part_1, part_2, part_3)
    part_in = (part_in_1, part_in_2, part_in_3)
    sums = (sums_1, sums_2, sums_3)
    sums_in = (sums_in_1, sums_in_2, sums_in_3)
    grads = (grads_1, grads_2, grads_3)
    x = lax.axis_index("dp")
    f = lax.axis_index("fsdp")
    c = f % 2
    y = (f // 2) % 8
    z = f // 16
    g = 2 * x + c
    other = 1 - c
    su = 2 + 14 * c
    sv = 16 - 14 * c
    pu = y + c * (z - y)
    pv = z + c * (y - z)
    sends = []

    def at(xx, ff):
        return {"dp": xx, "fsdp": ff}

    def mate(gg):
        return at(gg // 2, f - c + gg % 2)

    def dev_u(d):
        return at(x, ((pu + d + 8) % 8) * su + pv * sv + c)

    def dev_v(d):
        return at(x, pu * su + ((pv + d + 8) % 8) * sv + c)

    def dev_y(d):
        return at(x, z * 16 + ((y + d) % 8) * 2 + c)

    def dev_z(d):
        return at(x, ((z + d) % 8) * 16 + y * 2 + c)

    def dev_x(d):
        return at((x + d + 4) % 4, f)

    core = at(x, f - c + other)
    right = at(x, (f + 1) % 128)
    left = at(x, (f + 127) % 128)

    def copy(src, dst, ssem, rsem, dev):
        return pltpu.make_async_remote_copy(
            src_ref=src, dst_ref=dst, send_sem=ssem, recv_sem=rsem,
            device_id=dev, device_id_type=pl.DeviceIdType.MESH,
        )

    def send(src, dst, ssem, rsem, dev):
        one = copy(src, dst, ssem, rsem, dev)
        one.start()
        sends.append(one)

    def arrive(dst, ssem, rsem):
        copy(dst, dst, ssem, rsem, core).wait_recv()

    barrier = pltpu.get_barrier_semaphore()
    peers = [mate((g + r) % 8) for r in range(1, 8)]
    peers += [dev_y(r) for r in range(1, 8)] + [dev_z(r) for r in range(1, 8)] + [right, left]
    for dev in peers:
        pl.semaphore_signal(barrier, inc=1, device_id=dev, device_id_type=pl.DeviceIdType.MESH)

    tok = tok_ref[0].astype(F32)
    mean = jnp.mean(tok, axis=-1, keepdims=True)
    centered = tok - mean
    variance = jnp.mean(centered * centered, axis=-1, keepdims=True)
    scale = lax.rsqrt(variance + EPSILON)
    lane4 = lane_iota(4)
    extra = jnp.zeros((4, LANES), F32)
    for n, term in enumerate(three_terms(mean) + three_terms(scale)):
        extra = jnp.where((lane4 == n) | (lane4 == n + 8), term, extra)
    for b in range(8):
        for k in range(6):
            col = (6 * b + k) * LANES
            packed[32 * b + 4 * k : 32 * b + 4 * k + 4, :] = tok[:, col : col + LANES]
        packed[32 * b + 24 : 32 * b + 28, :] = extra
        packed[32 * b + 28 : 32 * b + 32, :] = jnp.zeros((4, LANES), F32)
    for b in range(8):
        letters[b] = packed[32 * b : 32 * b + 32, :].astype(BF16)

    pl.semaphore_wait(barrier, len(peers))
    for r in range(1, 8):
        gg = (g + r) % 8
        send(letters.at[gg], mail.at[g], mail_s.at[r - 1], mail_r.at[r - 1], mate(gg))
    mail[pl.ds(g, 1)] = letters[pl.ds(g, 1)]

    start = off_ref[f]
    length = off_ref[f + 1] - start
    shift_own = f * SHARD - start
    shift_right = shift_own + SHARD
    shift_left = shift_own - SHARD

    def widen(i, carry):
        rows = pl.ds(pl.multiple_of(i * 16, 16), 16)
        wide[pl.ds(pl.multiple_of(FRONT + i * 16, 16), 16), :] = slots_ref[rows, :].astype(F32)
        return carry

    lax.fori_loop(0, LINES // 16, widen, 0, unroll=8)

    def extract(first, shift, rows):
        turn = shift & (LANES - 1)
        row = FRONT + first + lax.shift_right_arithmetic(shift, 7)
        row = jnp.clip(row, 0, FRONT + LINES + BACK - rows - 1)
        here = wide[pl.ds(row, rows), :]
        after = wide[pl.ds(row + 1, rows), :]
        back = (LANES - turn) & (LANES - 1)
        lane = lane_iota(rows)
        line = lax.broadcasted_iota(jnp.int32, (rows, LANES), 0)
        moved = jnp.where(lane < LANES - turn, pltpu.roll(here, back, 1), pltpu.roll(after, back, 1))
        slot = (first + line) * LANES + lane + shift
        return jnp.where((slot >= 0) & (slot < length), moved, 0.0)

    def piece(piece_ref, first_row, rows, shift, top=None):
        def one(h, carry):
            got = extract((first_row + h) * 48 + 12 * x, shift, 16)
            lines[pl.ds(pl.multiple_of(h * 16, 16), 16), :] = got
            return carry

        lax.fori_loop(0, rows, one, 0, unroll=4)
        if top is not None:
            lines[0:1, :] = top
        for k in range(12):
            col = lines[pl.ds(k, rows, stride=16), :]
            piece_ref[k // 6, :, (k % 6) * LANES : (k % 6 + 1) * LANES] = col.astype(BF16)

    piece(left_out, 64, 32, shift_left, extract(0, shift_left + HID_DEV * D - 16, 8)[0:1])
    send(left_out, edge_left, edge_s.at[1], edge_r.at[1], left)
    piece(right_out, 0, 32, shift_right)
    send(right_out, edge_right, edge_s.at[0], edge_r.at[0], right)
    gain_own[...] = extract(0, shift_own + HID_DEV * D - 16, 8)

    for r in range(1, 8):
        arrive(mail.at[(g - r + 8) % 8], mail_s.at[r - 1], mail_r.at[r - 1])

    posts = mail[...].reshape(256, LANES)
    out_row = lax.broadcasted_iota(jnp.int32, (A_ROWS + B_ROWS, 256), 0)
    in_row = lax.broadcasted_iota(jnp.int32, (A_ROWS + B_ROWS, 256), 1)
    token = out_row & 31
    want = 32 * (token >> 2) + 4 * (out_row >> 5) + (token & 3)
    chunk = jnp.dot((want == in_row).astype(BF16), posts, preferred_element_type=F32)
    out_row = lax.broadcasted_iota(jnp.int32, (16, 256), 0) + 16
    in_row = lax.broadcasted_iota(jnp.int32, (16, 256), 1)
    want = 32 * (out_row >> 2) + 24 + (out_row & 3)
    late = jnp.dot((want == in_row).astype(BF16), posts, preferred_element_type=F32)
    lane = lane_iota(16)
    stats = jnp.where((lane >= 8) & (lane < 16), late, chunk[192:208])
    gath_a[0, 0] = chunk[0:A_ROWS].astype(BF16)
    gath_b[0, 0, 0:80, :] = chunk[A_ROWS:192].astype(BF16)
    gath_b[0, 0, 80:96, :] = stats.astype(BF16)

    for d in (1, -1, 2, -2, 3, -3, 4):
        n = SLOT[-d]
        send(gath_a.at[0, 0], gath_a.at[n, 0], one_s.at[0, n - 1], one_r.at[0, n - 1], dev_u(d))
        send(gath_b.at[0, 0], gath_b.at[0, n], one_s.at[1, n - 1], one_r.at[1, n - 1], dev_v(d))

    piece(own, 0, 96, shift_own)

    def unit_a(h, n):
        return gath_a.at[4 * h : 4 * h + 4, n]

    def unit_b(h, n):
        return gath_b.at[n, 4 * h : 4 * h + 4]

    streams = ((unit_a, dev_v, 1), (unit_a, dev_v, -1), (unit_b, dev_u, 1), (unit_b, dev_u, -1))

    def lands(s, h):
        for n, (unit, dev, d) in enumerate(streams):
            if s < 4 or (h == 0) == (d == 1):
                arrive(unit(h, SLOT[-d * s]), two_s.at[n, h, s - 1], two_r.at[n, h, s - 1])

    def onward(s, h):
        for n, (unit, dev, d) in enumerate(streams):
            if s < 4 or (h == 0) == (d == 1):
                send(
                    unit(h, SLOT[-d * (s - 1)]), unit(h, SLOT[-d * s]),
                    two_s.at[n, h, s - 1], two_r.at[n, h, s - 1], dev(d),
                )

    for n in (1, 2, 3):
        arrive(gath_a.at[n, 0], one_s.at[0, n - 1], one_r.at[0, n - 1])
        arrive(gath_b.at[0, n], one_s.at[1, n - 1], one_r.at[1, n - 1])
    onward(1, 0)
    for n in (4, 5, 6, 7):
        arrive(gath_a.at[n, 0], one_s.at[0, n - 1], one_r.at[0, n - 1])
        arrive(gath_b.at[0, n], one_s.at[1, n - 1], one_r.at[1, n - 1])
    onward(1, 1)

    arrive(edge_right, edge_s.at[0], edge_r.at[0])
    arrive(edge_left, edge_s.at[1], edge_r.at[1])
    row32 = lax.broadcasted_iota(jnp.int32, (32, BLOCK), 0)
    for half in range(2):
        spill[half, 0:32, :] = own[half, 0:32, :] + edge_right[half]
        spill[half, 32:64, :] = own[half, 32:64, :]
        low = jnp.where(row32 >= 8, edge_left[half].astype(F32), 0.0)
        spill[half, 64:96, :] = (own[half, 64:96, :].astype(F32) + low).astype(BF16)
        spill[half, 96:112, :] = jnp.zeros((16, BLOCK), BF16)
        first16 = edge_left[0, 0:16, 0:LANES].astype(F32)[0:8] + gain_own[...]
        lane8 = lane_iota(8)
        first16 = jnp.where((lane8 >= 16) & (lane8 < 64), first16, 0.0)
        first16 = jnp.concatenate([first16, jnp.zeros((8, LANES), F32)], axis=0)
        spill[half, 96:112, 0:LANES] = first16.astype(BF16)
    send(spill.at[other], weight.at[c], core_s.at[0], core_r.at[0], core)
    weight[pl.ds(c, 1)] = spill[pl.ds(c, 1)]

    lands(1, 0)
    onward(2, 0)

    arrive(weight.at[other], core_s.at[0], core_r.at[0])
    apart = (z - g + 8) % 8
    outs = [
        copy(gain_tiles.at[y], gain_tiles.at[y], gty_s.at[r - 1], gty_r.at[r - 1], dev_y(r)) for r in range(1, 8)
    ]

    @pl.when(apart == 0)
    def _():
        rows = jnp.concatenate(
            [weight[half, 96:112, 0:LANES].astype(F32)[0:1] for half in range(2)] + [jnp.zeros((6, LANES), F32)], axis=0
        )
        gain_tiles[pl.ds(y, 1)] = rows[None]
        for one in outs:
            one.start()

    lands(1, 1)
    onward(2, 1)

    t = lax.broadcasted_iota(jnp.int32, (1, 512), 1)
    home = (((z + 8 + away_ref[1:2, :]) & 7) * 8 + ((y + 8 + away_ref[0:1, :]) & 7)) * 8 + (t & 7)
    nat = lax.broadcasted_iota(jnp.int32, (512, 512), 0)
    cot[...] = jnp.dot(cot_ref[...], (nat == home).astype(BF16), preferred_element_type=F32)

    outs_z = [copy(gain_tiles, gain_tiles, gtz_s.at[r - 1], gtz_r, dev_z(r)) for r in range(1, 8)]

    @pl.when(apart == 0)
    def _():
        for r in range(1, 8):
            arrive(gain_tiles.at[(y - r + 8) % 8], gty_s.at[r - 1], gty_r.at[r - 1])
        for one in outs:
            one.wait_send()
        for one in outs_z:
            one.start()
        for one in outs_z:
            one.wait_send()

    lands(2, 0)
    onward(3, 0)

    @pl.when(apart != 0)
    def _():
        arrive(gain_tiles, gtz_s.at[0], gtz_r)

    for yy in range(8):
        gain_rows[2 * yy : 2 * yy + 2, :] = gain_tiles[yy, 0:2, :]
    spread = jnp.dot(gain_rows[...].astype(BF16), pick_ref[...], preferred_element_type=F32)
    gain = jnp.sum(spread * mask_ref[...], axis=0, keepdims=True)

    def normalize(first, places):
        data = []
        for a, b in places:
            uu, vv = a + c * (b - a), b + c * (a - b)
            rows = gath_b[uu, vv, 80:96, :].astype(F32)
            cols = []
            for base in (0, 3):
                early = (rows[:, base : base + 1] + rows[:, base + 1 : base + 2]) + rows[:, base + 2 : base + 3]
                late = (rows[:, base + 8 : base + 9] + rows[:, base + 9 : base + 10]) + rows[:, base + 10 : base + 11]
                cols.append((early[0:8], early[8:16], late[0:8], late[8:16]))
            data.append((uu, vv, cols))
        for k in range(6):
            gain_k = gain[:, k * LANES : (k + 1) * LANES]
            tiles = []
            for uu, vv, _ in data:
                if k < 3:
                    tile = gath_a[uu, vv, 32 * k : 32 * k + 32, :].astype(F32)
                elif k == 3:
                    tile = jnp.concatenate(
                        [gath_a[uu, vv, 96:112, :].astype(F32), gath_b[uu, vv, 0:16, :].astype(F32)], axis=0
                    )
                else:
                    tile = gath_b[uu, vv, 32 * k - 112 : 32 * k - 80, :].astype(F32)
                tiles.append(tile)
            for xx in range(4):
                both = jnp.concatenate(
                    [
                        (tiles[side][8 * xx : 8 * xx + 8] - data[side][2][0][xx]) * data[side][2][1][xx]
                        for side in range(2)
                    ],
                    axis=0,
                )
                rows = pl.ds(pl.multiple_of(512 * xx + 8 * first, 16), 16)
                norm[rows, k * LANES : (k + 1) * LANES] = both
                scaled[rows, k * LANES : (k + 1) * LANES] = (both * gain_k).astype(BF16)

    def pairs(low, high, first, place):
        def one(p, carry):
            normalize(first + 2 * p, (place(2 * p), place(2 * p + 1)))
            return carry

        lax.fori_loop(low, high, one, 0)

    block = weight[:, 0:96, :].reshape(192, BLOCK)

    def pre_act(n):
        low, size = SETS[n]
        for xx in range(4):
            got = lax.dot_general(
                block, scaled[512 * xx + low : 512 * xx + low + size, :], (((1,), (1,)), ((), ())),
                preferred_element_type=F32,
            )
            part[n][0, xx] = got[0:96]
            part[n][1, xx] = got[96:192]
        send(part[n].at[other], part_in[n], half_s.at[n], half_r.at[n], core)

    def sum_x(n):
        arrive(part_in[n], half_s.at[n], half_r.at[n])
        sums[n][...] = part[n][pl.ds(c, 1)][0] + part_in[n][...]
        for r in range(1, 4):
            send(sums[n].at[(x + r) % 4], sums_in[n].at[r - 1], sum_s.at[n, r - 1], sum_r.at[n, r - 1], dev_x(r))

    mine = pl.ds(pl.multiple_of(96 * c, 32), 96)
    theirs = pl.ds(pl.multiple_of(96 * other, 32), 96)

    def slope(n):
        low, size = SETS[n]
        for r in range(1, 4):
            arrive(sums_in[n].at[r - 1], sum_s.at[n, r - 1], sum_r.at[n, r - 1])
        total = (sums[n][pl.ds(x, 1)][0] + sums_in[n][0]) + (sums_in[n][1] + sums_in[n][2])
        grads[n][pl.ds(x, 1), mine, :] = (cot[:, low : low + size] * gelu_slope(total)).astype(BF16)[None]
        for r in range(1, 4):
            send(grads[n].at[x, mine], grads[n].at[x, mine], pg_s.at[n, r - 1], pg_r.at[n, r - 1], dev_x(r))

    def share(n):
        for r in range(1, 4):
            arrive(grads[n].at[(x - r + 4) % 4, mine], pg_s.at[n, r - 1], pg_r.at[n, r - 1])
        send(grads[n].at[:, mine], grads[n].at[:, mine], pgc_s.at[n], pgc_r.at[n], core)

    def shared(n):
        arrive(grads[n].at[:, theirs], pgc_s.at[n], pgc_r.at[n])

    def gradient(n):
        low, size = SETS[n]
        total = jnp.zeros((192, BLOCK), F32)
        for xx in range(4):
            rows = scaled[512 * xx + low : 512 * xx + low + size, :]
            total += jnp.dot(grads[n][xx], rows, preferred_element_type=F32)
        return total

    def gain_part(n):
        low, size = SETS[n]
        total = jnp.zeros((1, BLOCK), F32)
        for xx in range(4):
            back = lax.dot_general(grads[n][xx], block, (((0,), (0,)), ((), ())), preferred_element_type=F32)
            rows = norm[512 * xx + low : 512 * xx + low + size, :]
            total += jnp.sum(back * rows, axis=0, keepdims=True)
        return total

    pairs(0, 8, 0, lambda e: (e % 4, e // 4))
    pre_act(0)

    lands(2, 1)
    onward(3, 1)
    lands(3, 0)
    onward(4, 0)
    sum_x(0)
    lands(3, 1)
    onward(4, 1)

    pairs(0, 6, 16, lambda e: (4 + e % 3, e // 3))
    pairs(0, 10, 28, lambda e: (e % 7, 4 + e // 7))
    pre_act(1)
    slope(0)

    lands(4, 0)
    lands(4, 1)
    pairs(0, 4, 48, lambda e: (e, 7))
    pairs(4, 8, 48, lambda e: (7 - e // 15, e - 8 - e // 15))
    sum_x(1)
    pre_act(2)
    share(0)
    sum_x(2)
    shared(0)
    acc[...] = gradient(0)
    slope(1)
    gain_sum = gain_part(0)
    slope(2)
    share(1)
    share(2)
    shared(1)
    acc[...] += gradient(1)
    gain_sum += gain_part(1)
    shared(2)
    rounded = (acc[...] + gradient(2)).astype(BF16)

    block_out[0] = rounded[0:96]
    block_out[1] = rounded[96:192]
    send(block_out.at[other], result.at[x, c], core_s.at[1], core_r.at[1], core)
    result[pl.ds(x, 1), pl.ds(c, 1)] = block_out[pl.ds(c, 1)][None]
    for m, d in enumerate((1, -1)):
        send(result.at[x, c], result.at[x, c], res_s.at[m, 0], res_r.at[m, 0], dev_x(d))
    gain_sum += gain_part(2)
    for k in range(6):
        gain_mine[k : k + 1, :] = gain_sum[:, k * LANES : (k + 1) * LANES]
    gain_mine[6:8, :] = jnp.zeros((2, LANES), F32)
    arrive(result.at[x, other], core_s.at[1], core_r.at[1])
    for m, d in enumerate((1, -1)):
        send(result.at[x, other], result.at[x, other], res_s.at[m, 1], res_r.at[m, 1], dev_x(d))

    to_z = copy(gain_mine, gain_z.at[(apart + 7) % 8], gz_s, gz_r.at[(apart + 7) % 8], at(x, g * 16 + y * 2 + c))

    @pl.when(apart != 0)
    def _():
        to_z.start()

    def spell(xx, half):
        for k in range(6):
            col = result[xx, half, :, k * LANES : (k + 1) * LANES].astype(F32)
            out_ref[pl.ds(12 * xx + 6 * half + k, 96, stride=48), :] = col

    for half in range(2):
        spell(x, half)

    outs_y = [copy(gain_y.at[7], gain_y.at[r - 1], gy_s.at[r - 1], gy_r.at[r - 1], dev_y(r)) for r in range(1, 8)]

    @pl.when(apart == 0)
    def _():
        sum_z = gain_mine[...]
        for r in range(7):
            arrive(gain_z.at[r], gz_s, gz_r.at[r])
            sum_z += gain_z[r]
        gain_y[7] = sum_z
        for one in outs_y:
            one.start()

    arrive(result.at[(x + 3) % 4, c], res_s.at[0, 0], res_r.at[0, 0])
    arrive(result.at[(x + 1) % 4, c], res_s.at[1, 0], res_r.at[1, 0])
    arrive(result.at[(x + 3) % 4, other], res_s.at[0, 1], res_r.at[0, 1])
    send(result.at[(x + 3) % 4, 0], result.at[(x + 3) % 4, 0], res_s.at[0, 2], res_r.at[0, 2], dev_x(1))
    arrive(result.at[(x + 1) % 4, other], res_s.at[1, 1], res_r.at[1, 1])
    send(result.at[(x + 1) % 4, 1], result.at[(x + 1) % 4, 1], res_s.at[1, 2], res_r.at[1, 2], dev_x(-1))

    outs_f = [copy(gain_out, gain_out, gf_s.at[r - 1], gf_r, mate((g + r) % 8)) for r in range(1, 8)]

    @pl.when(apart == 0)
    def _():
        sum_y = gain_y[7]
        for r in range(7):
            arrive(gain_y.at[r], gy_s.at[r], gy_r.at[r])
            sum_y += gain_y[r]
        gain_out[...] = sum_y
        for one in outs_f:
            one.start()

    for half in range(2):
        spell((x + 3) % 4, half)
        spell((x + 1) % 4, half)

    @pl.when(apart != 0)
    def _():
        arrive(gain_out, gf_s.at[0], gf_r)
        to_z.wait_send()

    @pl.when(apart == 0)
    def _():
        for one in outs_y:
            one.wait_send()
        for one in outs_f:
            one.wait_send()

    first = 48 * (2 * y + c)
    turn = first % LANES
    line = first // LANES
    here = jnp.broadcast_to(gain_out[pl.ds(line, 1), :], (8, LANES))
    after = jnp.broadcast_to(gain_out[pl.ds(line + 1, 1), :], (8, LANES))
    back = (LANES - turn) % LANES
    moved = jnp.where(lane_iota(8) < LANES - turn, pltpu.roll(here, back, 1), pltpu.roll(after, back, 1))
    out_ref[4608:4616, :] = moved

    arrive(result.at[(x + 2) % 4, 0], res_s.at[0, 2], res_r.at[0, 2])
    spell((x + 2) % 4, 0)
    arrive(result.at[(x + 2) % 4, 1], res_s.at[1, 2], res_r.at[1, 2])
    spell((x + 2) % 4, 1)
    for one in sends:
        one.wait_send()


def body(tokens, act_cot, old_slots, offsets):
    vmem = pl.BlockSpec(memory_space=pltpu.VMEM)
    smem = pl.BlockSpec(memory_space=pltpu.SMEM)
    dma = pltpu.SemaphoreType.DMA
    slots = jnp.pad(old_slots, (0, LINES * LANES - old_slots.shape[0])).reshape(LINES, LANES)
    chips = chips_in_order()
    away = np.array([[AWAY[chip[axis]] for chip in chips for _ in range(8)] for axis in range(2)], np.int32)
    n = np.arange(BLOCK)
    lanes = np.arange(LANES)[:, None]
    pick = jnp.asarray((lanes == 16 + n % 48).astype(np.float32), BF16)
    mask = jnp.asarray((np.arange(16)[:, None] == n // 48).astype(np.float32))
    out = pl.pallas_call(
        main_kernel,
        out_shape=jax.ShapeDtypeStruct((4616, LANES), F32),
        in_specs=[vmem, vmem, smem, vmem, vmem, vmem, vmem],
        out_specs=vmem,
        scratch_shapes=[
            pltpu.VMEM((FRONT + LINES + BACK, LANES), F32),
            pltpu.VMEM((96 * 16, LANES), F32),
            pltpu.VMEM((256, LANES), F32),
            pltpu.VMEM((8, 32, LANES), BF16),
            pltpu.VMEM((8, 32, LANES), BF16),
            pltpu.VMEM((2, 96, BLOCK), BF16),
            pltpu.VMEM((2, 32, BLOCK), BF16),
            pltpu.VMEM((2, 32, BLOCK), BF16),
            pltpu.VMEM((2, 32, BLOCK), BF16),
            pltpu.VMEM((2, 32, BLOCK), BF16),
            pltpu.VMEM((2, 112, BLOCK), BF16),
            pltpu.VMEM((2, 112, BLOCK), BF16),
            pltpu.VMEM((8, 8, A_ROWS, LANES), BF16),
            pltpu.VMEM((8, 8, B_ROWS, LANES), BF16),
            pltpu.VMEM((96, 512), F32),
            pltpu.VMEM((2048, BLOCK), F32),
            pltpu.VMEM((2048, BLOCK), BF16),
            *[pltpu.VMEM((2, 4, 96, size), F32) for _, size in SETS],
            *[pltpu.VMEM((4, 96, size), F32) for _, size in SETS],
            *[pltpu.VMEM((4, 96, size), F32) for _, size in SETS],
            *[pltpu.VMEM((3, 96, size), F32) for _, size in SETS],
            *[pltpu.VMEM((4, 192, size), BF16) for _, size in SETS],
            pltpu.VMEM((192, BLOCK), F32),
            pltpu.VMEM((4, 2, 96, BLOCK), BF16),
            pltpu.VMEM((2, 96, BLOCK), BF16),
            pltpu.VMEM((8, LANES), F32),
            pltpu.VMEM((8, 8, LANES), F32),
            pltpu.VMEM((16, LANES), F32),
            pltpu.VMEM((8, LANES), F32),
            pltpu.VMEM((8, 8, LANES), F32),
            pltpu.VMEM((8, 8, LANES), F32),
            pltpu.VMEM((8, LANES), F32),
            dma((7,)), dma((7,)),
            dma((2,)), dma((2,)),
            dma((2,)), dma((2,)),
            dma((2, 7)), dma((2, 7)),
            dma((4, 2, 4)), dma((4, 2, 4)),
            dma((3,)), dma((3,)),
            dma((3, 3)), dma((3, 3)),
            dma((3, 3)), dma((3, 3)),
            dma((3,)), dma((3,)),
            dma((2, 3)), dma((2, 3)),
            dma((7,)), dma((7,)),
            dma((7,)), dma,
            dma, dma((8,)),
            dma((7,)), dma((7,)),
            dma((7,)), dma,
        ],
        compiler_params=pltpu.CompilerParams(
            collective_id=0, has_side_effects=True, vmem_limit_bytes=56 * 2**20
        ),
    )(tokens, slots, offsets, act_cot[0].T, jnp.asarray(away), pick, mask)
    return out.reshape(-1)[:SHARD]


def solution(mesh):
    placed = (P("dp", "fsdp", None), P("dp", None, "fsdp"), P("fsdp"), P())
    return jax.shard_map(body, mesh=mesh, in_specs=placed, out_specs=P("fsdp"), check_vma=False)
```

```python
import jax
import jax.numpy as jnp
import numpy as np
from jax import lax
from jax.experimental import pallas as pl
from jax.experimental.pallas import tpu as pltpu
from jax.sharding import PartitionSpec as P

D = 6144
HID_DEV = 96
SHARD = 589872
EPSILON = 1e-06
LINES = 6928
FRONT = 2704
BACK = 384
BLOCK = 768
LANES = 128
A_ROWS = 112
B_ROWS = 96
F32 = jnp.float32
BF16 = jnp.bfloat16
AWAY = (0, 1, -1, 2, -2, 3, -3, 4)
SLOT = {d: n for n, d in enumerate(AWAY)}
SLOT[-4] = SLOT[4]
SETS = ((0, 128), (128, 256), (384, 128))


def chips_in_order():
    near = [(a, b) for b in range(4) for a in range(4)]
    mid = [(4 + e % 3, e // 3) for e in range(12)] + [(e % 7, 4 + e // 7) for e in range(20)]
    far = [(e, 7) for e in range(8)] + [(7 - e // 15, e - 8 - e // 15) for e in range(8, 16)]
    return near + mid + far


def lane_iota(rows):
    return lax.broadcasted_iota(jnp.int32, (rows, LANES), 1)


def three_terms(value):
    high = value.astype(BF16).astype(F32)
    rest = value - high
    mid = rest.astype(BF16).astype(F32)
    return high, mid, rest - mid


def gelu_slope(v):
    root = 0.7978845608028654
    t = jnp.tanh(root * (v + 0.044715 * (v * v * v)))
    return 0.5 * (1.0 + t) + 0.5 * v * (1.0 - t * t) * (root * (1.0 + 3 * 0.044715 * (v * v)))


def main_kernel(
    tok_ref, slots_ref, off_ref, cot_ref, away_ref, pick_ref, mask_ref, out_ref,
    wide, lines, packed, letters, mail, own, right_out, left_out, edge_right, edge_left,
    spill, weight, gain_pair, gath_a, gath_b, cot, norm, scaled,
    part_1, part_2, part_3, part_in_1, part_in_2, part_in_3,
    sums_1, sums_2, sums_3, sums_in_1, sums_in_2, sums_in_3, grads_1, grads_2, grads_3,
    acc, result, block_out, gain_own, gain_tiles, gain_rows, gain_mine, gain_z, gain_y, gain_out,
    mail_s, mail_r, edge_s, edge_r, core_s, core_r, one_s, one_r, two_s, two_r,
    half_s, half_r, sum_s, sum_r, pg_s, pg_r, pgc_s, pgc_r, res_s, res_r,
    gty_s, gty_r, gtz_s, gtz_r, gz_s, gz_r, gy_s, gy_r, gf_s, gf_r,
):
    part = (part_1, part_2, part_3)
    part_in = (part_in_1, part_in_2, part_in_3)
    sums = (sums_1, sums_2, sums_3)
    sums_in = (sums_in_1, sums_in_2, sums_in_3)
    grads = (grads_1, grads_2, grads_3)
    x = lax.axis_index("dp")
    f = lax.axis_index("fsdp")
    c = f % 2
    y = (f // 2) % 8
    z = f // 16
    g = 2 * x + c
    other = 1 - c
    su = 2 + 14 * c
    sv = 16 - 14 * c
    pu = y + c * (z - y)
    pv = z + c * (y - z)
    sends = []

    def at(xx, ff):
        return {"dp": xx, "fsdp": ff}

    def mate(gg):
        return at(gg // 2, f - c + gg % 2)

    def dev_u(d):
        return at(x, ((pu + d + 8) % 8) * su + pv * sv + c)

    def dev_v(d):
        return at(x, pu * su + ((pv + d + 8) % 8) * sv + c)

    def dev_y(d):
        return at(x, z * 16 + ((y + d) % 8) * 2 + c)

    def dev_z(d):
        return at(x, ((z + d) % 8) * 16 + y * 2 + c)

    def dev_x(d):
        return at((x + d + 4) % 4, f)

    core = at(x, f - c + other)
    right = at(x, (f + 1) % 128)
    left = at(x, (f + 127) % 128)

    def copy(src, dst, ssem, rsem, dev):
        return pltpu.make_async_remote_copy(
            src_ref=src, dst_ref=dst, send_sem=ssem, recv_sem=rsem,
            device_id=dev, device_id_type=pl.DeviceIdType.MESH,
        )

    def send(src, dst, ssem, rsem, dev):
        one = copy(src, dst, ssem, rsem, dev)
        one.start()
        sends.append(one)

    def arrive(dst, ssem, rsem):
        copy(dst, dst, ssem, rsem, core).wait_recv()

    barrier = pltpu.get_barrier_semaphore()
    peers = [mate((g + r) % 8) for r in range(1, 8)]
    peers += [dev_y(r) for r in range(1, 8)] + [dev_z(r) for r in range(1, 8)] + [right, left]
    for dev in peers:
        pl.semaphore_signal(barrier, inc=1, device_id=dev, device_id_type=pl.DeviceIdType.MESH)

    tok = tok_ref[0].astype(F32)
    mean = jnp.mean(tok, axis=-1, keepdims=True)
    centered = tok - mean
    variance = jnp.mean(centered * centered, axis=-1, keepdims=True)
    scale = lax.rsqrt(variance + EPSILON)
    lane4 = lane_iota(4)
    extra = jnp.zeros((4, LANES), F32)
    for n, term in enumerate(three_terms(mean) + three_terms(scale)):
        extra = jnp.where((lane4 == n) | (lane4 == n + 8), term, extra)
    for b in range(8):
        for k in range(6):
            col = (6 * b + k) * LANES
            packed[32 * b + 4 * k : 32 * b + 4 * k + 4, :] = tok[:, col : col + LANES]
        packed[32 * b + 24 : 32 * b + 28, :] = extra
        packed[32 * b + 28 : 32 * b + 32, :] = jnp.zeros((4, LANES), F32)
    for b in range(8):
        letters[b] = packed[32 * b : 32 * b + 32, :].astype(BF16)

    pl.semaphore_wait(barrier, len(peers))
    for r in range(1, 8):
        gg = (g + r) % 8
        send(letters.at[gg], mail.at[g], mail_s.at[r - 1], mail_r.at[r - 1], mate(gg))
    mail[pl.ds(g, 1)] = letters[pl.ds(g, 1)]

    start = off_ref[f]
    length = off_ref[f + 1] - start
    shift_own = f * SHARD - start
    shift_right = shift_own + SHARD
    shift_left = shift_own - SHARD

    def widen(i, carry):
        rows = pl.ds(pl.multiple_of(i * 16, 16), 16)
        wide[pl.ds(pl.multiple_of(FRONT + i * 16, 16), 16), :] = slots_ref[rows, :].astype(F32)
        return carry

    lax.fori_loop(0, LINES // 16, widen, 0, unroll=8)

    def extract(first, shift, rows):
        turn = shift & (LANES - 1)
        row = FRONT + first + lax.shift_right_arithmetic(shift, 7)
        row = jnp.clip(row, 0, FRONT + LINES + BACK - rows - 1)
        here = wide[pl.ds(row, rows), :]
        after = wide[pl.ds(row + 1, rows), :]
        back = (LANES - turn) & (LANES - 1)
        lane = lane_iota(rows)
        line = lax.broadcasted_iota(jnp.int32, (rows, LANES), 0)
        moved = jnp.where(lane < LANES - turn, pltpu.roll(here, back, 1), pltpu.roll(after, back, 1))
        slot = (first + line) * LANES + lane + shift
        return jnp.where((slot >= 0) & (slot < length), moved, 0.0)

    def move(first_row, low, high, shift):
        def one(h, carry):
            got = extract((first_row + h) * 48 + 12 * x, shift, 16)
            lines[pl.ds(pl.multiple_of(h * 16, 16), 16), :] = got
            return carry

        lax.fori_loop(low, high, one, 0, unroll=4)

    def keep(piece_ref, rows):
        for k in range(12):
            col = lines[pl.ds(k, rows, stride=16), :]
            piece_ref[k // 6, :, (k % 6) * LANES : (k % 6 + 1) * LANES] = col.astype(BF16)

    move(64, 0, 32, shift_left)
    lines[0:1, :] = extract(0, shift_left + HID_DEV * D - 16, 8)[0:1]
    keep(left_out, 32)
    send(left_out, edge_left, edge_s.at[1], edge_r.at[1], left)
    move(0, 0, 32, shift_right)
    keep(right_out, 32)
    send(right_out, edge_right, edge_s.at[0], edge_r.at[0], right)
    gain_own[...] = extract(0, shift_own + HID_DEV * D - 16, 8)

    for r in range(1, 8):
        arrive(mail.at[(g - r + 8) % 8], mail_s.at[r - 1], mail_r.at[r - 1])

    posts = mail[...].reshape(256, LANES)
    out_row = lax.broadcasted_iota(jnp.int32, (A_ROWS + B_ROWS, 256), 0)
    in_row = lax.broadcasted_iota(jnp.int32, (A_ROWS + B_ROWS, 256), 1)
    token = out_row & 31
    want = 32 * (token >> 2) + 4 * (out_row >> 5) + (token & 3)
    chunk = jnp.dot((want == in_row).astype(BF16), posts, preferred_element_type=F32)
    out_row = lax.broadcasted_iota(jnp.int32, (16, 256), 0) + 16
    in_row = lax.broadcasted_iota(jnp.int32, (16, 256), 1)
    want = 32 * (out_row >> 2) + 24 + (out_row & 3)
    late = jnp.dot((want == in_row).astype(BF16), posts, preferred_element_type=F32)
    lane = lane_iota(16)
    stats = jnp.where((lane >= 8) & (lane < 16), late, chunk[192:208])
    gath_a[0, 0] = chunk[0:A_ROWS].astype(BF16)
    gath_b[0, 0, 0:80, :] = chunk[A_ROWS:192].astype(BF16)
    gath_b[0, 0, 80:96, :] = stats.astype(BF16)

    for d in (1, -1, 2, -2, 3, -3, 4):
        n = SLOT[-d]
        send(gath_a.at[0, 0], gath_a.at[n, 0], one_s.at[0, n - 1], one_r.at[0, n - 1], dev_u(d))
        send(gath_b.at[0, 0], gath_b.at[0, n], one_s.at[1, n - 1], one_r.at[1, n - 1], dev_v(d))

    move(0, 0, 32, shift_own)
    arrive(edge_left, edge_s.at[1], edge_r.at[1])
    lane8 = lane_iota(8)
    gain_row = edge_left[0, 0:16, 0:LANES].astype(F32)[0:8] + gain_own[...]
    gain_pair[pl.ds(c, 1)] = jnp.where((lane8 >= 16) & (lane8 < 64), gain_row, 0.0)[None]
    send(gain_pair.at[c], gain_pair.at[c], core_s.at[2], core_r.at[2], core)
    move(0, 32, 64, shift_own)
    arrive(gain_pair.at[other], core_s.at[2], core_r.at[2])
    apart = (z - g + 8) % 8
    outs = [
        copy(gain_tiles.at[y], gain_tiles.at[y], gty_s.at[r - 1], gty_r.at[r - 1], dev_y(r)) for r in range(1, 8)
    ]

    @pl.when(apart == 0)
    def _():
        rows = jnp.concatenate([gain_pair[0, 0:1], gain_pair[1, 0:1], jnp.zeros((6, LANES), F32)], axis=0)
        gain_tiles[pl.ds(y, 1)] = rows[None]
        for one in outs:
            one.start()

    def unit_a(h, n):
        return gath_a.at[2 * h : 2 * h + 2, n]

    def unit_b(h, n):
        return gath_b.at[n, 2 * h : 2 * h + 2]

    streams = ((unit_a, dev_v, 1), (unit_a, dev_v, -1), (unit_b, dev_u, 1), (unit_b, dev_u, -1))

    def lands(s, h):
        for n, (unit, dev, d) in enumerate(streams):
            if s < 4 or (h < 2) == (d == 1):
                arrive(unit(h, SLOT[-d * s]), two_s.at[n, h, s - 1], two_r.at[n, h, s - 1])

    def onward(s, h):
        if s > 1:
            lands(s - 1, h)
        for n, (unit, dev, d) in enumerate(streams):
            if s < 4 or (h < 2) == (d == 1):
                send(
                    unit(h, SLOT[-d * (s - 1)]), unit(h, SLOT[-d * s]),
                    two_s.at[n, h, s - 1], two_r.at[n, h, s - 1], dev(d),
                )

    def first_axis(n):
        arrive(gath_a.at[n, 0], one_s.at[0, n - 1], one_r.at[0, n - 1])
        arrive(gath_b.at[0, n], one_s.at[1, n - 1], one_r.at[1, n - 1])

    first_axis(1)
    onward(1, 0)
    first_axis(2)
    first_axis(3)
    onward(1, 1)
    move(0, 64, 96, shift_own)
    first_axis(4)
    first_axis(5)
    onward(1, 2)
    first_axis(6)
    first_axis(7)
    onward(1, 3)

    keep(own, 96)
    arrive(edge_right, edge_s.at[0], edge_r.at[0])
    row32 = lax.broadcasted_iota(jnp.int32, (32, BLOCK), 0)
    for half in range(2):
        spill[half, 0:32, :] = own[half, 0:32, :] + edge_right[half]
        spill[half, 32:64, :] = own[half, 32:64, :]
        low = jnp.where(row32 >= 8, edge_left[half].astype(F32), 0.0)
        spill[half, 64:96, :] = (own[half, 64:96, :].astype(F32) + low).astype(BF16)
    send(spill.at[other], weight.at[c], core_s.at[0], core_r.at[0], core)
    weight[pl.ds(c, 1)] = spill[pl.ds(c, 1)]
    onward(2, 0)

    def reorder(low):
        t = lax.broadcasted_iota(jnp.int32, (1, 256), 1)
        away_y, away_z = away_ref[0:1, low : low + 256], away_ref[1:2, low : low + 256]
        home = (((z + 8 + away_z) & 7) * 8 + ((y + 8 + away_y) & 7)) * 8 + (t & 7)
        nat = lax.broadcasted_iota(jnp.int32, (512, 256), 0)
        cot[:, low : low + 256] = jnp.dot(cot_ref[...], (nat == home).astype(BF16), preferred_element_type=F32)

    reorder(0)
    onward(2, 1)
    reorder(256)
    onward(2, 2)
    outs_z = [copy(gain_tiles, gain_tiles, gtz_s.at[r - 1], gtz_r, dev_z(r)) for r in range(1, 8)]

    @pl.when(apart == 0)
    def _():
        for r in range(1, 8):
            arrive(gain_tiles.at[(y - r + 8) % 8], gty_s.at[r - 1], gty_r.at[r - 1])
        for one in outs:
            one.wait_send()
        for one in outs_z:
            one.start()

    onward(2, 3)
    arrive(weight.at[other], core_s.at[0], core_r.at[0])
    onward(3, 0)
    onward(3, 1)

    @pl.when(apart != 0)
    def _():
        arrive(gain_tiles, gtz_s.at[0], gtz_r)

    @pl.when(apart == 0)
    def _():
        for one in outs_z:
            one.wait_send()

    for yy in range(8):
        gain_rows[2 * yy : 2 * yy + 2, :] = gain_tiles[yy, 0:2, :]
    spread = jnp.dot(gain_rows[...].astype(BF16), pick_ref[...], preferred_element_type=F32)
    gain = jnp.sum(spread * mask_ref[...], axis=0, keepdims=True)

    def normalize(first, places):
        data = []
        for a, b in places:
            uu, vv = a + c * (b - a), b + c * (a - b)
            rows = gath_b[uu, vv, 80:96, :].astype(F32)
            cols = []
            for base in (0, 3):
                early = (rows[:, base : base + 1] + rows[:, base + 1 : base + 2]) + rows[:, base + 2 : base + 3]
                late = (rows[:, base + 8 : base + 9] + rows[:, base + 9 : base + 10]) + rows[:, base + 10 : base + 11]
                cols.append((early[0:8], early[8:16], late[0:8], late[8:16]))
            data.append((uu, vv, cols))
        for k in range(6):
            gain_k = gain[:, k * LANES : (k + 1) * LANES]
            tiles = []
            for uu, vv, _ in data:
                if k < 3:
                    tile = gath_a[uu, vv, 32 * k : 32 * k + 32, :].astype(F32)
                elif k == 3:
                    tile = jnp.concatenate(
                        [gath_a[uu, vv, 96:112, :].astype(F32), gath_b[uu, vv, 0:16, :].astype(F32)], axis=0
                    )
                else:
                    tile = gath_b[uu, vv, 32 * k - 112 : 32 * k - 80, :].astype(F32)
                tiles.append(tile)
            for xx in range(4):
                both = jnp.concatenate(
                    [
                        (tiles[side][8 * xx : 8 * xx + 8] - data[side][2][0][xx]) * data[side][2][1][xx]
                        for side in range(2)
                    ],
                    axis=0,
                )
                rows = pl.ds(pl.multiple_of(512 * xx + 8 * first, 16), 16)
                norm[rows, k * LANES : (k + 1) * LANES] = both
                scaled[rows, k * LANES : (k + 1) * LANES] = (both * gain_k).astype(BF16)

    def pairs(low, high, first, place):
        def one(p, carry):
            normalize(first + 2 * p, (place(2 * p), place(2 * p + 1)))
            return carry

        lax.fori_loop(low, high, one, 0)

    block = weight[...].reshape(192, BLOCK)

    def pre_act(n):
        low, size = SETS[n]
        for xx in range(4):
            got = lax.dot_general(
                block, scaled[512 * xx + low : 512 * xx + low + size, :], (((1,), (1,)), ((), ())),
                preferred_element_type=F32,
            )
            part[n][0, xx] = got[0:96]
            part[n][1, xx] = got[96:192]
        send(part[n].at[other], part_in[n], half_s.at[n], half_r.at[n], core)

    def sum_x(n):
        arrive(part_in[n], half_s.at[n], half_r.at[n])
        sums[n][...] = part[n][pl.ds(c, 1)][0] + part_in[n][...]
        for r in range(1, 4):
            send(sums[n].at[(x + r) % 4], sums_in[n].at[r - 1], sum_s.at[n, r - 1], sum_r.at[n, r - 1], dev_x(r))

    mine = pl.ds(pl.multiple_of(96 * c, 32), 96)
    theirs = pl.ds(pl.multiple_of(96 * other, 32), 96)

    def slope(n):
        low, size = SETS[n]
        for r in range(1, 4):
            arrive(sums_in[n].at[r - 1], sum_s.at[n, r - 1], sum_r.at[n, r - 1])
        total = (sums[n][pl.ds(x, 1)][0] + sums_in[n][0]) + (sums_in[n][1] + sums_in[n][2])
        grads[n][pl.ds(x, 1), mine, :] = (cot[:, low : low + size] * gelu_slope(total)).astype(BF16)[None]
        for r in range(1, 4):
            send(grads[n].at[x, mine], grads[n].at[x, mine], pg_s.at[n, r - 1], pg_r.at[n, r - 1], dev_x(r))

    def share(n):
        for r in range(1, 4):
            arrive(grads[n].at[(x - r + 4) % 4, mine], pg_s.at[n, r - 1], pg_r.at[n, r - 1])
        send(grads[n].at[:, mine], grads[n].at[:, mine], pgc_s.at[n], pgc_r.at[n], core)

    def shared(n):
        arrive(grads[n].at[:, theirs], pgc_s.at[n], pgc_r.at[n])

    def gradient(n):
        low, size = SETS[n]
        total = jnp.zeros((192, BLOCK), F32)
        for xx in range(4):
            rows = scaled[512 * xx + low : 512 * xx + low + size, :]
            total += jnp.dot(grads[n][xx], rows, preferred_element_type=F32)
        return total

    def gain_part(n):
        low, size = SETS[n]
        total = jnp.zeros((1, BLOCK), F32)
        for xx in range(4):
            back = lax.dot_general(grads[n][xx], block, (((0,), (0,)), ((), ())), preferred_element_type=F32)
            rows = norm[512 * xx + low : 512 * xx + low + size, :]
            total += jnp.sum(back * rows, axis=0, keepdims=True)
        return total

    def near(low, high):
        pairs(low, high, 0, lambda e: (e % 4, e // 4))

    def mid_a(low, high):
        pairs(low, high, 16, lambda e: (4 + e % 3, e // 3))

    def mid_b(low, high):
        pairs(low, high, 28, lambda e: (e % 7, 4 + e // 7))

    near(0, 4)
    onward(3, 2)
    near(4, 8)
    onward(3, 3)
    pre_act(0)
    onward(4, 0)
    sum_x(0)
    onward(4, 1)
    mid_a(0, 3)
    onward(4, 2)
    mid_a(3, 6)
    onward(4, 3)
    mid_b(0, 10)
    pre_act(1)
    slope(0)
    sum_x(1)
    for h in range(4):
        lands(4, h)
    pairs(0, 4, 48, lambda e: (e, 7))
    pairs(4, 8, 48, lambda e: (7 - e // 15, e - 8 - e // 15))
    pre_act(2)
    share(0)
    sum_x(2)
    slope(1)
    shared(0)
    acc[...] = gradient(0)
    gain_sum = gain_part(0)
    slope(2)
    share(1)
    shared(1)
    acc[...] += gradient(1)
    gain_sum += gain_part(1)
    share(2)
    shared(2)
    rounded = (acc[...] + gradient(2)).astype(BF16)

    block_out[0] = rounded[0:96]
    block_out[1] = rounded[96:192]
    send(block_out.at[other], result.at[x, c], core_s.at[1], core_r.at[1], core)
    result[pl.ds(x, 1), pl.ds(c, 1)] = block_out[pl.ds(c, 1)][None]
    for m, d in enumerate((1, -1)):
        send(result.at[x, c], result.at[x, c], res_s.at[m, 0], res_r.at[m, 0], dev_x(d))
    gain_sum += gain_part(2)
    for k in range(6):
        gain_mine[k : k + 1, :] = gain_sum[:, k * LANES : (k + 1) * LANES]
    gain_mine[6:8, :] = jnp.zeros((2, LANES), F32)
    arrive(result.at[x, other], core_s.at[1], core_r.at[1])
    for m, d in enumerate((1, -1)):
        send(result.at[x, other], result.at[x, other], res_s.at[m, 1], res_r.at[m, 1], dev_x(d))

    to_z = copy(gain_mine, gain_z.at[(apart + 7) % 8], gz_s, gz_r.at[(apart + 7) % 8], at(x, g * 16 + y * 2 + c))

    @pl.when(apart != 0)
    def _():
        to_z.start()

    def spell(xx, half):
        for k in range(6):
            col = result[xx, half, :, k * LANES : (k + 1) * LANES].astype(F32)
            out_ref[pl.ds(12 * xx + 6 * half + k, 96, stride=48), :] = col

    for half in range(2):
        spell(x, half)

    outs_y = [copy(gain_y.at[7], gain_y.at[r - 1], gy_s.at[r - 1], gy_r.at[r - 1], dev_y(r)) for r in range(1, 8)]

    @pl.when(apart == 0)
    def _():
        sum_z = gain_mine[...]
        for r in range(7):
            arrive(gain_z.at[r], gz_s, gz_r.at[r])
            sum_z += gain_z[r]
        gain_y[7] = sum_z
        for one in outs_y:
            one.start()

    arrive(result.at[(x + 3) % 4, c], res_s.at[0, 0], res_r.at[0, 0])
    arrive(result.at[(x + 1) % 4, c], res_s.at[1, 0], res_r.at[1, 0])
    arrive(result.at[(x + 3) % 4, other], res_s.at[0, 1], res_r.at[0, 1])
    send(result.at[(x + 3) % 4, 0], result.at[(x + 3) % 4, 0], res_s.at[0, 2], res_r.at[0, 2], dev_x(1))
    arrive(result.at[(x + 1) % 4, other], res_s.at[1, 1], res_r.at[1, 1])
    send(result.at[(x + 1) % 4, 1], result.at[(x + 1) % 4, 1], res_s.at[1, 2], res_r.at[1, 2], dev_x(-1))

    outs_f = [copy(gain_out, gain_out, gf_s.at[r - 1], gf_r, mate((g + r) % 8)) for r in range(1, 8)]

    @pl.when(apart == 0)
    def _():
        sum_y = gain_y[7]
        for r in range(7):
            arrive(gain_y.at[r], gy_s.at[r], gy_r.at[r])
            sum_y += gain_y[r]
        gain_out[...] = sum_y
        for one in outs_f:
            one.start()

    for half in range(2):
        spell((x + 3) % 4, half)
        spell((x + 1) % 4, half)

    @pl.when(apart != 0)
    def _():
        arrive(gain_out, gf_s.at[0], gf_r)
        to_z.wait_send()

    @pl.when(apart == 0)
    def _():
        for one in outs_y:
            one.wait_send()
        for one in outs_f:
            one.wait_send()

    first = 48 * (2 * y + c)
    turn = first % LANES
    line = first // LANES
    here = jnp.broadcast_to(gain_out[pl.ds(line, 1), :], (8, LANES))
    after = jnp.broadcast_to(gain_out[pl.ds(line + 1, 1), :], (8, LANES))
    back = (LANES - turn) % LANES
    moved = jnp.where(lane_iota(8) < LANES - turn, pltpu.roll(here, back, 1), pltpu.roll(after, back, 1))
    out_ref[4608:4616, :] = moved

    arrive(result.at[(x + 2) % 4, 0], res_s.at[0, 2], res_r.at[0, 2])
    spell((x + 2) % 4, 0)
    arrive(result.at[(x + 2) % 4, 1], res_s.at[1, 2], res_r.at[1, 2])
    spell((x + 2) % 4, 1)
    for one in sends:
        one.wait_send()


def body(tokens, act_cot, old_slots, offsets):
    vmem = pl.BlockSpec(memory_space=pltpu.VMEM)
    smem = pl.BlockSpec(memory_space=pltpu.SMEM)
    dma = pltpu.SemaphoreType.DMA
    slots = jnp.pad(old_slots, (0, LINES * LANES - old_slots.shape[0])).reshape(LINES, LANES)
    chips = chips_in_order()
    away = np.array([[AWAY[chip[axis]] for chip in chips for _ in range(8)] for axis in range(2)], np.int32)
    n = np.arange(BLOCK)
    lanes = np.arange(LANES)[:, None]
    pick = jnp.asarray((lanes == 16 + n % 48).astype(np.float32), BF16)
    mask = jnp.asarray((np.arange(16)[:, None] == n // 48).astype(np.float32))
    out = pl.pallas_call(
        main_kernel,
        out_shape=jax.ShapeDtypeStruct((4616, LANES), F32),
        in_specs=[vmem, vmem, smem, vmem, vmem, vmem, vmem],
        out_specs=vmem,
        scratch_shapes=[
            pltpu.VMEM((FRONT + LINES + BACK, LANES), F32),
            pltpu.VMEM((96 * 16, LANES), F32),
            pltpu.VMEM((256, LANES), F32),
            pltpu.VMEM((8, 32, LANES), BF16),
            pltpu.VMEM((8, 32, LANES), BF16),
            pltpu.VMEM((2, 96, BLOCK), BF16),
            pltpu.VMEM((2, 32, BLOCK), BF16),
            pltpu.VMEM((2, 32, BLOCK), BF16),
            pltpu.VMEM((2, 32, BLOCK), BF16),
            pltpu.VMEM((2, 32, BLOCK), BF16),
            pltpu.VMEM((2, 96, BLOCK), BF16),
            pltpu.VMEM((2, 96, BLOCK), BF16),
            pltpu.VMEM((2, 8, LANES), F32),
            pltpu.VMEM((8, 8, A_ROWS, LANES), BF16),
            pltpu.VMEM((8, 8, B_ROWS, LANES), BF16),
            pltpu.VMEM((96, 512), F32),
            pltpu.VMEM((2048, BLOCK), F32),
            pltpu.VMEM((2048, BLOCK), BF16),
            *[pltpu.VMEM((2, 4, 96, size), F32) for _, size in SETS],
            *[pltpu.VMEM((4, 96, size), F32) for _, size in SETS],
            *[pltpu.VMEM((4, 96, size), F32) for _, size in SETS],
            *[pltpu.VMEM((3, 96, size), F32) for _, size in SETS],
            *[pltpu.VMEM((4, 192, size), BF16) for _, size in SETS],
            pltpu.VMEM((192, BLOCK), F32),
            pltpu.VMEM((4, 2, 96, BLOCK), BF16),
            pltpu.VMEM((2, 96, BLOCK), BF16),
            pltpu.VMEM((8, LANES), F32),
            pltpu.VMEM((8, 8, LANES), F32),
            pltpu.VMEM((16, LANES), F32),
            pltpu.VMEM((8, LANES), F32),
            pltpu.VMEM((8, 8, LANES), F32),
            pltpu.VMEM((8, 8, LANES), F32),
            pltpu.VMEM((8, LANES), F32),
            dma((7,)), dma((7,)),
            dma((2,)), dma((2,)),
            dma((3,)), dma((3,)),
            dma((2, 7)), dma((2, 7)),
            dma((4, 4, 4)), dma((4, 4, 4)),
            dma((3,)), dma((3,)),
            dma((3, 3)), dma((3, 3)),
            dma((3, 3)), dma((3, 3)),
            dma((3,)), dma((3,)),
            dma((2, 3)), dma((2, 3)),
            dma((7,)), dma((7,)),
            dma((7,)), dma,
            dma, dma((8,)),
            dma((7,)), dma((7,)),
            dma((7,)), dma,
        ],
        compiler_params=pltpu.CompilerParams(
            collective_id=0, has_side_effects=True, vmem_limit_bytes=40 * 2**20
        ),
    )(tokens, slots, offsets, act_cot[0].T, jnp.asarray(away), pick, mask)
    return out.reshape(-1)[:SHARD]


def solution(mesh):
    placed = (P("dp", "fsdp", None), P("dp", None, "fsdp"), P("fsdp"), P())
    return jax.shard_map(body, mesh=mesh, in_specs=placed, out_specs=P("fsdp"), check_vma=False)
```

```python
import jax
import jax.numpy as jnp
import numpy as np
from jax import lax
from jax.experimental import pallas as pl
from jax.experimental.pallas import tpu as pltpu
from jax.sharding import PartitionSpec as P

D = 6144
HID_DEV = 96
SHARD = 589872
EPSILON = 1e-06
LINES = 6928
FRONT = 2320
BACK = 64
BLOCK = 768
LANES = 128
A_ROWS = 112
B_ROWS = 96
F32 = jnp.float32
BF16 = jnp.bfloat16
AWAY = (0, 1, -1, 2, -2, 3, -3, 4)
SLOT = {d: n for n, d in enumerate(AWAY)}
SLOT[-4] = SLOT[4]
SETS = 4
SIZE = 128


def chips_in_order():
    return [place(e) for place in (near, side, corner, far) for e in range(16)]


def near(e):
    return e % 4, e // 4


def side(e):
    beyond = e // 12
    return (1 - beyond) * (4 + e % 3) + beyond * (e - 12), (1 - beyond) * (e // 3) + beyond * 4


def corner(e):
    beyond = e // 8
    return (1 - beyond) * (e % 4) + beyond * (4 + (e - 8) % 3), (1 - beyond) * (5 + e // 4) + beyond * (4 + (e - 8) // 3)


def far(e):
    beyond = e // 8
    last = e // 15
    return (1 - beyond) * e + beyond * (7 - last), (1 - beyond) * 7 + beyond * (e - 8 - last)


def lane_iota(rows):
    return lax.broadcasted_iota(jnp.int32, (rows, LANES), 1)


def three_terms(value):
    high = value.astype(BF16).astype(F32)
    rest = value - high
    mid = rest.astype(BF16).astype(F32)
    return high, mid, rest - mid


def gelu_slope(v):
    root = 0.7978845608028654
    t = jnp.tanh(root * (v + 0.044715 * (v * v * v)))
    return 0.5 * (1.0 + t) + 0.5 * v * (1.0 - t * t) * (root * (1.0 + 3 * 0.044715 * (v * v)))


def main_kernel(
    tok_ref, slots_ref, off_ref, cot_ref, away_ref, pick_ref, mask_ref, out_ref,
    wide, lines, packed, letters, mail, own, right_out, left_out, edge_right, edge_left,
    spill, weight, gain_pair, gath_a, gath_b, cot, norm, scaled,
    part, part_in, sums, sums_in, grads,
    acc, result, block_out, gain_own, gain_left, gain_right, gain_tiles, gain_rows, gain_mine, gain_z, gain_y, gain_out,
    mail_s, mail_r, edge_s, edge_r, core_s, core_r, one_s, one_r, two_s, two_r,
    half_s, half_r, sum_s, sum_r, pg_s, pg_r, pgc_s, pgc_r, last_s, last_r, direct_s, direct_r, res_s, res_r,
    gty_s, gty_r, gtz_s, gtz_r, gz_s, gz_r, gy_s, gy_r, gf_s, gf_r,
):
    x = lax.axis_index("dp")
    f = lax.axis_index("fsdp")
    c = f % 2
    y = (f // 2) % 8
    z = f // 16
    g = 2 * x + c
    other = 1 - c
    su = 2 + 14 * c
    sv = 16 - 14 * c
    pu = y + c * (z - y)
    pv = z + c * (y - z)
    sends = []

    def at(xx, ff):
        return {"dp": xx, "fsdp": ff}

    def mate(gg):
        return at(gg // 2, f - c + gg % 2)

    def dev_u(d):
        return at(x, ((pu + d + 8) % 8) * su + pv * sv + c)

    def dev_v(d):
        return at(x, pu * su + ((pv + d + 8) % 8) * sv + c)

    def dev_y(d):
        return at(x, z * 16 + ((y + d) % 8) * 2 + c)

    def dev_z(d):
        return at(x, ((z + d) % 8) * 16 + y * 2 + c)

    def dev_x(d):
        return at((x + d + 4) % 4, f)

    core = at(x, f - c + other)
    right = at(x, (f + 1) % 128)
    left = at(x, (f + 127) % 128)

    def copy(src, dst, ssem, rsem, dev):
        return pltpu.make_async_remote_copy(
            src_ref=src, dst_ref=dst, send_sem=ssem, recv_sem=rsem,
            device_id=dev, device_id_type=pl.DeviceIdType.MESH,
        )

    def send(src, dst, ssem, rsem, dev):
        one = copy(src, dst, ssem, rsem, dev)
        one.start()
        sends.append(one)

    def arrive(dst, ssem, rsem):
        copy(dst, dst, ssem, rsem, core).wait_recv()

    barrier = pltpu.get_barrier_semaphore()
    peers = [mate((g + r) % 8) for r in range(1, 8)]
    peers += [dev_y(r) for r in range(1, 8)] + [dev_z(r) for r in range(1, 8)] + [right, left]
    for dev in peers:
        pl.semaphore_signal(barrier, inc=1, device_id=dev, device_id_type=pl.DeviceIdType.MESH)

    tok = tok_ref[0].astype(F32)
    mean = jnp.mean(tok, axis=-1, keepdims=True)
    centered = tok - mean
    variance = jnp.mean(centered * centered, axis=-1, keepdims=True)
    scale = lax.rsqrt(variance + EPSILON)
    lane4 = lane_iota(4)
    extra = jnp.zeros((4, LANES), F32)
    for n, term in enumerate(three_terms(mean) + three_terms(scale)):
        extra = jnp.where((lane4 == n) | (lane4 == n + 8), term, extra)
    for b in range(8):
        for k in range(6):
            col = (6 * b + k) * LANES
            packed[32 * b + 4 * k : 32 * b + 4 * k + 4, :] = tok[:, col : col + LANES]
        packed[32 * b + 24 : 32 * b + 28, :] = extra
        packed[32 * b + 28 : 32 * b + 32, :] = jnp.zeros((4, LANES), F32)
    for b in range(8):
        letters[b] = packed[32 * b : 32 * b + 32, :].astype(BF16)

    pl.semaphore_wait(barrier, len(peers))
    for r in range(1, 8):
        gg = (g + r) % 8
        send(letters.at[gg], mail.at[g], mail_s.at[r - 1], mail_r.at[r - 1], mate(gg))
    mail[pl.ds(g, 1)] = letters[pl.ds(g, 1)]

    start = off_ref[f]
    length = off_ref[f + 1] - start
    shift_own = f * SHARD - start
    shift_right = shift_own + SHARD
    shift_left = shift_own - SHARD

    line16 = lax.broadcasted_iota(jnp.int32, (16, LANES), 0) * LANES + lane_iota(16)

    def widen(i, carry):
        rows = pl.ds(pl.multiple_of(i * 16, 16), 16)
        valid = line16 < length - i * (16 * LANES)
        wide[pl.ds(pl.multiple_of(FRONT + i * 16, 16), 16), :] = jnp.where(valid, slots_ref[rows, :].astype(F32), 0.0)
        return carry

    wide[0:FRONT, :] = jnp.zeros((FRONT, LANES), F32)
    wide[FRONT + LINES :, :] = jnp.zeros((BACK, LANES), F32)
    lax.fori_loop(0, LINES // 16, widen, 0, unroll=8)

    def turned(first, shift, rows):
        row = FRONT + first + lax.shift_right_arithmetic(shift, 7)
        row = jnp.clip(row, 0, FRONT + LINES + BACK - rows)
        back = (LANES - (shift & (LANES - 1))) & (LANES - 1)
        return pltpu.roll(wide[pl.ds(row, rows), :], back, 1)

    def before_cut(rows, shift):
        return lane_iota(rows) < LANES - (shift & (LANES - 1))

    def line_of(shift):
        got = turned(0, shift, 8)
        return jnp.where(before_cut(1, shift), got[0:1], got[1:2])

    def move(first_row, low, high, shift):
        def one(h, carry):
            lines[pl.ds(pl.multiple_of(h * 16, 16), 16), :] = turned((first_row + h) * 48 + 12 * x, shift, 16)
            return carry

        lax.fori_loop(low, high, one, 0, unroll=8)

    def keep(piece_ref, rows, shift):
        mask = before_cut(rows, shift)
        here = lines[pl.ds(0, rows, stride=16), :]
        for k in range(12):
            after = lines[pl.ds(k + 1, rows, stride=16), :]
            piece_ref[k // 6, :, (k % 6) * LANES : (k % 6 + 1) * LANES] = jnp.where(mask, here, after).astype(BF16)
            here = after

    gain_row = jnp.broadcast_to(line_of(shift_left + HID_DEV * D - 16), (8, LANES))
    gain_left[...] = gain_row
    send(gain_left, gain_right, core_s.at[3], core_r.at[3], left)
    gain_own[...] = jnp.broadcast_to(line_of(shift_own + HID_DEV * D - 16), (8, LANES))
    lines[0:128, :] = jnp.zeros((128, LANES), F32)
    move(64, 8, 32, shift_left)
    keep(left_out, 32, shift_left)
    send(left_out, edge_left, edge_s.at[1], edge_r.at[1], left)
    move(0, 0, 25, shift_right)
    lines[400:512, :] = jnp.zeros((112, LANES), F32)
    keep(right_out, 32, shift_right)
    send(right_out, edge_right, edge_s.at[0], edge_r.at[0], right)

    for r in range(1, 8):
        arrive(mail.at[(g - r + 8) % 8], mail_s.at[r - 1], mail_r.at[r - 1])

    posts = mail[...].reshape(256, LANES)
    out_row = lax.broadcasted_iota(jnp.int32, (A_ROWS + B_ROWS, 256), 0)
    in_row = lax.broadcasted_iota(jnp.int32, (A_ROWS + B_ROWS, 256), 1)
    token = out_row & 31
    want = 32 * (token >> 2) + 4 * (out_row >> 5) + (token & 3)
    chunk = jnp.dot((want == in_row).astype(BF16), posts, preferred_element_type=F32)
    out_row = lax.broadcasted_iota(jnp.int32, (16, 256), 0) + 16
    in_row = lax.broadcasted_iota(jnp.int32, (16, 256), 1)
    want = 32 * (out_row >> 2) + 24 + (out_row & 3)
    late = jnp.dot((want == in_row).astype(BF16), posts, preferred_element_type=F32)
    lane = lane_iota(16)
    stats = jnp.where((lane >= 8) & (lane < 16), late, chunk[192:208])
    gath_a[0, 0] = chunk[0:A_ROWS].astype(BF16)
    gath_b[0, 0, 0:80, :] = chunk[A_ROWS:192].astype(BF16)
    gath_b[0, 0, 80:96, :] = stats.astype(BF16)

    for d in (1, -1, 2, -2, 3, -3, 4):
        n = SLOT[-d]
        send(gath_a.at[0, 0], gath_a.at[n, 0], one_s.at[0, n - 1], one_r.at[0, n - 1], dev_u(d))
        send(gath_b.at[0, 0], gath_b.at[0, n], one_s.at[1, n - 1], one_r.at[1, n - 1], dev_v(d))

    move(0, 0, 96, shift_own)
    keep(own, 96, shift_own)
    arrive(gain_right, core_s.at[3], core_r.at[3])
    lane8 = lane_iota(8)
    gain_row = jnp.where((lane8 >= 16) & (lane8 < 64), gain_right[...] + gain_own[...], 0.0)
    gain_pair[pl.ds(c, 1)] = gain_row[None]
    send(gain_pair.at[c], gain_pair.at[c], core_s.at[2], core_r.at[2], core)
    apart = (z - g + 8) % 8

    def unit_a(h, n):
        return gath_a.at[2 * h : 2 * h + 2, n]

    def unit_b(h, n):
        return gath_b.at[n, 2 * h : 2 * h + 2]

    streams = ((unit_a, dev_v, 1), (unit_a, dev_v, -1), (unit_b, dev_u, 1), (unit_b, dev_u, -1))

    def lands(s, h):
        for n, (unit, dev, d) in enumerate(streams):
            if s < 4 or (h < 2) == (d == 1):
                arrive(unit(h, SLOT[-d * s]), two_s.at[n, h, s - 1], two_r.at[n, h, s - 1])

    def onward(s, h):
        if s > 1:
            lands(s - 1, h)
        for n, (unit, dev, d) in enumerate(streams):
            if s < 4 or (h < 2) == (d == 1):
                send(
                    unit(h, SLOT[-d * (s - 1)]), unit(h, SLOT[-d * s]),
                    two_s.at[n, h, s - 1], two_r.at[n, h, s - 1], dev(d),
                )

    def first_axis(n):
        arrive(gath_a.at[n, 0], one_s.at[0, n - 1], one_r.at[0, n - 1])
        arrive(gath_b.at[0, n], one_s.at[1, n - 1], one_r.at[1, n - 1])

    first_axis(1)
    onward(1, 0)
    arrive(gain_pair.at[other], core_s.at[2], core_r.at[2])
    outs = [
        copy(gain_tiles.at[y], gain_tiles.at[y], gty_s.at[r - 1], gty_r.at[r - 1], dev_y(r)) for r in range(1, 8)
    ]

    @pl.when(apart == 0)
    def _():
        rows = jnp.concatenate([gain_pair[0, 0:1], gain_pair[1, 0:1], jnp.zeros((6, LANES), F32)], axis=0)
        gain_tiles[pl.ds(y, 1)] = rows[None]
        for one in outs:
            one.start()

    first_axis(2)
    first_axis(3)
    onward(1, 1)
    first_axis(4)
    first_axis(5)
    onward(1, 2)
    first_axis(6)
    first_axis(7)
    onward(1, 3)

    arrive(edge_left, edge_s.at[1], edge_r.at[1])
    arrive(edge_right, edge_s.at[0], edge_r.at[0])
    for half in range(2):
        spill[half, 0:32, :] = own[half, 0:32, :] + edge_right[half]
        spill[half, 32:64, :] = own[half, 32:64, :]
        spill[half, 64:96, :] = own[half, 64:96, :] + edge_left[half]
    send(spill.at[other], weight.at[c], core_s.at[0], core_r.at[0], core)
    weight[pl.ds(c, 1)] = spill[pl.ds(c, 1)]
    onward(2, 0)

    def reorder(low):
        t = lax.broadcasted_iota(jnp.int32, (1, 256), 1)
        away_y, away_z = away_ref[0:1, low : low + 256], away_ref[1:2, low : low + 256]
        home = (((z + 8 + away_z) & 7) * 8 + ((y + 8 + away_y) & 7)) * 8 + (t & 7)
        nat = lax.broadcasted_iota(jnp.int32, (512, 256), 0)
        cot[:, low : low + 256] = jnp.dot(cot_ref[...], (nat == home).astype(BF16), preferred_element_type=F32)

    reorder(0)
    onward(2, 1)
    reorder(256)
    onward(2, 2)
    outs_z = [copy(gain_tiles, gain_tiles, gtz_s.at[r - 1], gtz_r, dev_z(r)) for r in range(1, 8)]

    @pl.when(apart == 0)
    def _():
        for r in range(1, 8):
            arrive(gain_tiles.at[(y - r + 8) % 8], gty_s.at[r - 1], gty_r.at[r - 1])
        for one in outs:
            one.wait_send()
        for one in outs_z:
            one.start()

    onward(2, 3)
    arrive(weight.at[other], core_s.at[0], core_r.at[0])
    onward(3, 0)
    onward(3, 1)

    @pl.when(apart != 0)
    def _():
        arrive(gain_tiles, gtz_s.at[0], gtz_r)

    @pl.when(apart == 0)
    def _():
        for one in outs_z:
            one.wait_send()

    for yy in range(8):
        gain_rows[2 * yy : 2 * yy + 2, :] = gain_tiles[yy, 0:2, :]
    spread = jnp.dot(gain_rows[...].astype(BF16), pick_ref[...], preferred_element_type=F32)
    gain = jnp.sum(spread * mask_ref[...], axis=0, keepdims=True)

    def normalize(first, places):
        data = []
        for a, b in places:
            uu, vv = a + c * (b - a), b + c * (a - b)
            rows = gath_b[uu, vv, 80:96, :].astype(F32)
            cols = []
            for base in (0, 3):
                early = (rows[:, base : base + 1] + rows[:, base + 1 : base + 2]) + rows[:, base + 2 : base + 3]
                late = (rows[:, base + 8 : base + 9] + rows[:, base + 9 : base + 10]) + rows[:, base + 10 : base + 11]
                cols.append((early[0:8], early[8:16], late[0:8], late[8:16]))
            data.append((uu, vv, cols))
        for k in range(6):
            gain_k = gain[:, k * LANES : (k + 1) * LANES]
            tiles = []
            for uu, vv, _ in data:
                if k < 3:
                    tile = gath_a[uu, vv, 32 * k : 32 * k + 32, :].astype(F32)
                elif k == 3:
                    tile = jnp.concatenate(
                        [gath_a[uu, vv, 96:112, :].astype(F32), gath_b[uu, vv, 0:16, :].astype(F32)], axis=0
                    )
                else:
                    tile = gath_b[uu, vv, 32 * k - 112 : 32 * k - 80, :].astype(F32)
                tiles.append(tile)
            for xx in range(4):
                both = jnp.concatenate(
                    [
                        (tiles[side][8 * xx : 8 * xx + 8] - data[side][2][0][xx]) * data[side][2][1][xx]
                        for side in range(2)
                    ],
                    axis=0,
                )
                rows = pl.ds(512 * xx + 8 * first, 16)
                norm[rows, k * LANES : (k + 1) * LANES] = both
                scaled[rows, k * LANES : (k + 1) * LANES] = (both * gain_k).astype(BF16)

    def pairs(n, place, low=0, high=16):
        for e in range(low, high, 2):
            normalize(16 * n + e, (place(e), place(e + 1)))

    block = weight[...].reshape(192, BLOCK)

    def rows_of(n, xx):
        return slice(512 * xx + SIZE * n, 512 * xx + SIZE * (n + 1))

    def pre_act(n):
        for xx in range(4):
            got = lax.dot_general(
                block, scaled[rows_of(n, xx), :], (((1,), (1,)), ((), ())), preferred_element_type=F32
            )
            part[n, 0, xx] = got[0:96]
            part[n, 1, xx] = got[96:192]
        send(part.at[n, other], part_in.at[n], half_s.at[n], half_r.at[n], core)

    def sum_x(n):
        arrive(part_in.at[n], half_s.at[n], half_r.at[n])
        sums[n] = part[n, pl.ds(c, 1)][0] + part_in[n]
        for r in range(1, 4):
            send(sums.at[n, (x + r) % 4], sums_in.at[n, r - 1], sum_s.at[n, r - 1], sum_r.at[n, r - 1], dev_x(r))

    def last_pre_act(n):
        for r in (2, 1, 3, 0):
            xx = (x + r) % 4
            rows = scaled[pl.ds(pl.multiple_of(512 * xx + SIZE * n, SIZE), SIZE), :]
            got = lax.dot_general(block, rows, (((1,), (1,)), ((), ())), preferred_element_type=F32)
            part[n, 0, pl.ds(xx, 1)] = got[0:96][None]
            part[n, 1, pl.ds(xx, 1)] = got[96:192][None]
            send(part.at[n, other, xx], part_in.at[n, xx], last_s.at[r], last_r.at[r], core)

    def last_sum_x(n):
        for r in (2, 1, 3, 0):
            xx = (x + r) % 4
            arrive(part_in.at[n, xx], last_s.at[r], last_r.at[r])
            sums[n, pl.ds(xx, 1)] = part[n, pl.ds(c, 1), pl.ds(xx, 1)][0] + part_in[n, pl.ds(xx, 1)]
            if r:
                send(sums.at[n, xx], sums_in.at[n, r - 1], sum_s.at[n, r - 1], sum_r.at[n, r - 1], dev_x(r))

    mine = pl.ds(pl.multiple_of(96 * c, 32), 96)
    theirs = pl.ds(pl.multiple_of(96 * other, 32), 96)

    def slope(n):
        for r in range(1, 4):
            arrive(sums_in.at[n, r - 1], sum_s.at[n, r - 1], sum_r.at[n, r - 1])
        total = (sums[n, pl.ds(x, 1)][0] + sums_in[n, 0]) + (sums_in[n, 1] + sums_in[n, 2])
        got = (cot[:, SIZE * n : SIZE * (n + 1)] * gelu_slope(total)).astype(BF16)
        grads[n, pl.ds(x, 1), mine, :] = got[None]
        if n == SETS - 1:
            for r in (4, 5, 3, 2, 6, 1, 7):
                send(grads.at[n, x, mine], grads.at[n, x, mine], direct_s.at[r - 1], direct_r.at[r - 1], mate((g + r) % 8))
        else:
            for r in range(1, 4):
                send(grads.at[n, x, mine], grads.at[n, x, mine], pg_s.at[n, r - 1], pg_r.at[n, r - 1], dev_x(r))

    def last_shared(n):
        for r in range(1, 8):
            gg = (g - r + 8) % 8
            rows = pl.ds(pl.multiple_of(96 * (gg % 2), 32), 96)
            arrive(grads.at[n, gg // 2, rows], direct_s.at[r - 1], direct_r.at[r - 1])

    def share(n):
        for r in range(1, 4):
            arrive(grads.at[n, (x - r + 4) % 4, mine], pg_s.at[n, r - 1], pg_r.at[n, r - 1])
        send(grads.at[n, :, mine], grads.at[n, :, mine], pgc_s.at[n], pgc_r.at[n], core)

    def shared(n):
        arrive(grads.at[n, :, theirs], pgc_s.at[n], pgc_r.at[n])

    def gradient(n):
        total = jnp.zeros((192, BLOCK), F32)
        for xx in range(4):
            total += jnp.dot(grads[n, xx], scaled[rows_of(n, xx), :], preferred_element_type=F32)
        return total

    def gain_part(n):
        total = jnp.zeros((1, BLOCK), F32)
        for xx in range(4):
            back = lax.dot_general(grads[n, xx], block, (((0,), (0,)), ((), ())), preferred_element_type=F32)
            total += jnp.sum(back * norm[rows_of(n, xx), :], axis=0, keepdims=True)
        return total

    pairs(0, near)
    pre_act(0)
    onward(3, 2)
    sum_x(0)
    onward(3, 3)
    onward(4, 0)
    onward(4, 1)
    pairs(1, side)
    pre_act(1)
    onward(4, 2)
    sum_x(1)
    pairs(2, corner, 0, 8)
    onward(4, 3)
    pairs(2, corner, 8, 16)
    pre_act(2)
    sum_x(2)
    slope(0)
    for h in range(4):
        lands(4, h)
    pairs(3, far)
    last_pre_act(3)
    last_sum_x(3)
    slope(1)
    share(0)
    shared(0)
    acc[...] = gradient(0)
    gain_sum = gain_part(0)
    slope(2)
    share(1)
    slope(3)
    shared(1)
    acc[...] += gradient(1)
    gain_sum += gain_part(1)
    share(2)
    shared(2)
    acc[...] += gradient(2)
    gain_sum += gain_part(2)
    last_shared(3)
    rounded = (acc[...] + gradient(3)).astype(BF16)

    block_out[0] = rounded[0:96]
    block_out[1] = rounded[96:192]
    send(block_out.at[other], result.at[x, c], core_s.at[1], core_r.at[1], core)
    result[pl.ds(x, 1), pl.ds(c, 1)] = block_out[pl.ds(c, 1)][None]
    way = 1 - 2 * c
    send(result.at[x, c], result.at[x, c], res_s.at[c, 0], res_r.at[c, 0], dev_x(way))
    arrive(result.at[x, other], core_s.at[1], core_r.at[1])
    send(result.at[x, other], result.at[x, other], res_s.at[other, 0], res_r.at[other, 0], dev_x(-way))
    send(result.at[x, other], result.at[x, other], res_s.at[c, 1], res_r.at[c, 1], dev_x(way))
    send(result.at[x, c], result.at[x, c], res_s.at[other, 1], res_r.at[other, 1], dev_x(-way))
    gain_sum += gain_part(3)
    for k in range(6):
        gain_mine[k : k + 1, :] = gain_sum[:, k * LANES : (k + 1) * LANES]
    gain_mine[6:8, :] = jnp.zeros((2, LANES), F32)

    to_z = copy(gain_mine, gain_z.at[(apart + 7) % 8], gz_s, gz_r.at[(apart + 7) % 8], at(x, g * 16 + y * 2 + c))

    @pl.when(apart != 0)
    def _():
        to_z.start()

    def spell(xx, half):
        for k in range(6):
            col = result[xx, half, :, k * LANES : (k + 1) * LANES].astype(F32)
            out_ref[pl.ds(12 * xx + 6 * half + k, 96, stride=48), :] = col

    for half in range(2):
        spell(x, half)

    outs_y = [copy(gain_y.at[7], gain_y.at[r - 1], gy_s.at[r - 1], gy_r.at[r - 1], dev_y(r)) for r in range(1, 8)]

    @pl.when(apart == 0)
    def _():
        sum_z = gain_mine[...]
        for r in range(7):
            arrive(gain_z.at[r], gz_s, gz_r.at[r])
            sum_z += gain_z[r]
        gain_y[7] = sum_z
        for one in outs_y:
            one.start()

    for m, d in enumerate((1, -1)):
        arrive(result.at[(x - d + 4) % 4, m], res_s.at[m, 0], res_r.at[m, 0])
        send(result.at[(x - d + 4) % 4, m], result.at[(x - d + 4) % 4, m], res_s.at[m, 2], res_r.at[m, 2], dev_x(d))

    outs_f = [copy(gain_out, gain_out, gf_s.at[r - 1], gf_r, mate((g + r) % 8)) for r in range(1, 8)]

    @pl.when(apart == 0)
    def _():
        sum_y = gain_y[7]
        for r in range(7):
            arrive(gain_y.at[r], gy_s.at[r], gy_r.at[r])
            sum_y += gain_y[r]
        gain_out[...] = sum_y
        for one in outs_f:
            one.start()

    for m, d in enumerate((1, -1)):
        spell((x - d + 4) % 4, m)
    for m, d in enumerate((1, -1)):
        arrive(result.at[(x - d + 4) % 4, 1 - m], res_s.at[m, 1], res_r.at[m, 1])
        spell((x - d + 4) % 4, 1 - m)

    @pl.when(apart != 0)
    def _():
        arrive(gain_out, gf_s.at[0], gf_r)
        to_z.wait_send()

    @pl.when(apart == 0)
    def _():
        for one in outs_y:
            one.wait_send()
        for one in outs_f:
            one.wait_send()

    first = 48 * (2 * y + c)
    turn = first % LANES
    line = first // LANES
    here = jnp.broadcast_to(gain_out[pl.ds(line, 1), :], (8, LANES))
    after = jnp.broadcast_to(gain_out[pl.ds(line + 1, 1), :], (8, LANES))
    back = (LANES - turn) % LANES
    moved = jnp.where(lane_iota(8) < LANES - turn, pltpu.roll(here, back, 1), pltpu.roll(after, back, 1))
    out_ref[4608:4616, :] = moved

    arrive(result.at[(x + 2) % 4, 0], res_s.at[0, 2], res_r.at[0, 2])
    spell((x + 2) % 4, 0)
    arrive(result.at[(x + 2) % 4, 1], res_s.at[1, 2], res_r.at[1, 2])
    spell((x + 2) % 4, 1)
    for one in sends:
        one.wait_send()


def body(tokens, act_cot, old_slots, offsets):
    vmem = pl.BlockSpec(memory_space=pltpu.VMEM)
    smem = pl.BlockSpec(memory_space=pltpu.SMEM)
    dma = pltpu.SemaphoreType.DMA
    slots = jnp.pad(old_slots, (0, LINES * LANES - old_slots.shape[0])).reshape(LINES, LANES)
    chips = chips_in_order()
    away = np.array([[AWAY[chip[axis]] for chip in chips for _ in range(8)] for axis in range(2)], np.int32)
    n = np.arange(BLOCK)
    lanes = np.arange(LANES)[:, None]
    pick = jnp.asarray((lanes == 16 + n % 48).astype(np.float32), BF16)
    mask = jnp.asarray((np.arange(16)[:, None] == n // 48).astype(np.float32))
    out = pl.pallas_call(
        main_kernel,
        out_shape=jax.ShapeDtypeStruct((4616, LANES), F32),
        in_specs=[vmem, vmem, smem, vmem, vmem, vmem, vmem],
        out_specs=vmem,
        scratch_shapes=[
            pltpu.VMEM((FRONT + LINES + BACK, LANES), F32),
            pltpu.VMEM((96 * 16, LANES), F32),
            pltpu.VMEM((256, LANES), F32),
            pltpu.VMEM((8, 32, LANES), BF16),
            pltpu.VMEM((8, 32, LANES), BF16),
            pltpu.VMEM((2, 96, BLOCK), BF16),
            pltpu.VMEM((2, 32, BLOCK), BF16),
            pltpu.VMEM((2, 32, BLOCK), BF16),
            pltpu.VMEM((2, 32, BLOCK), BF16),
            pltpu.VMEM((2, 32, BLOCK), BF16),
            pltpu.VMEM((2, 96, BLOCK), BF16),
            pltpu.VMEM((2, 96, BLOCK), BF16),
            pltpu.VMEM((2, 8, LANES), F32),
            pltpu.VMEM((8, 8, A_ROWS, LANES), BF16),
            pltpu.VMEM((8, 8, B_ROWS, LANES), BF16),
            pltpu.VMEM((96, 512), F32),
            pltpu.VMEM((2048, BLOCK), F32),
            pltpu.VMEM((2048, BLOCK), BF16),
            pltpu.VMEM((SETS, 2, 4, 96, SIZE), F32),
            pltpu.VMEM((SETS, 4, 96, SIZE), F32),
            pltpu.VMEM((SETS, 4, 96, SIZE), F32),
            pltpu.VMEM((SETS, 3, 96, SIZE), F32),
            pltpu.VMEM((SETS, 4, 192, SIZE), BF16),
            pltpu.VMEM((192, BLOCK), F32),
            pltpu.VMEM((4, 2, 96, BLOCK), BF16),
            pltpu.VMEM((2, 96, BLOCK), BF16),
            pltpu.VMEM((8, LANES), F32),
            pltpu.VMEM((8, LANES), F32),
            pltpu.VMEM((8, LANES), F32),
            pltpu.VMEM((8, 8, LANES), F32),
            pltpu.VMEM((16, LANES), F32),
            pltpu.VMEM((8, LANES), F32),
            pltpu.VMEM((8, 8, LANES), F32),
            pltpu.VMEM((8, 8, LANES), F32),
            pltpu.VMEM((8, LANES), F32),
            dma((7,)), dma((7,)),
            dma((2,)), dma((2,)),
            dma((4,)), dma((4,)),
            dma((2, 7)), dma((2, 7)),
            dma((4, 4, 4)), dma((4, 4, 4)),
            dma((SETS,)), dma((SETS,)),
            dma((SETS, 3)), dma((SETS, 3)),
            dma((SETS, 3)), dma((SETS, 3)),
            dma((SETS,)), dma((SETS,)),
            dma((4,)), dma((4,)),
            dma((7,)), dma((7,)),
            dma((2, 3)), dma((2, 3)),
            dma((7,)), dma((7,)),
            dma((7,)), dma,
            dma, dma((8,)),
            dma((7,)), dma((7,)),
            dma((7,)), dma,
        ],
        compiler_params=pltpu.CompilerParams(
            collective_id=0, has_side_effects=True, vmem_limit_bytes=40 * 2**20
        ),
    )(tokens, slots, offsets, act_cot[0].T, jnp.asarray(away), pick, mask)
    return out.reshape(-1)[:SHARD]


def solution(mesh):
    placed = (P("dp", "fsdp", None), P("dp", None, "fsdp"), P("fsdp"), P())
    return jax.shard_map(body, mesh=mesh, in_specs=placed, out_specs=P("fsdp"), check_vma=False)
```

```python
import jax
import jax.numpy as jnp
import numpy as np
from jax import lax
from jax.experimental import pallas as pl
from jax.experimental.pallas import tpu as pltpu
from jax.sharding import PartitionSpec as P

D = 6144
HID_DEV = 96
SHARD = 589872
EPSILON = 1e-06
LINES = 6928
FRONT = 2320
BACK = 64
BLOCK = 768
LANES = 128
A_ROWS = 112
B_ROWS = 96
F32 = jnp.float32
BF16 = jnp.bfloat16
AWAY = (0, 1, -1, 2, -2, 3, -3, 4)
SLOT = {d: n for n, d in enumerate(AWAY)}
SLOT[-4] = SLOT[4]
SETS = 4
SIZE = 128


def chips_in_order():
    return [place(e) for place in (near, side, corner, far) for e in range(16)]


def near(e):
    return e % 4, e // 4


def side(e):
    beyond = e // 12
    return (1 - beyond) * (4 + e % 3) + beyond * (e - 12), (1 - beyond) * (e // 3) + beyond * 4


def corner(e):
    beyond = e // 8
    return (1 - beyond) * (e % 4) + beyond * (4 + (e - 8) % 3), (1 - beyond) * (5 + e // 4) + beyond * (4 + (e - 8) // 3)


def far(e):
    beyond = e // 8
    last = e // 15
    return (1 - beyond) * e + beyond * (7 - last), (1 - beyond) * 7 + beyond * (e - 8 - last)


def lane_iota(rows):
    return lax.broadcasted_iota(jnp.int32, (rows, LANES), 1)


def three_terms(value):
    high = value.astype(BF16).astype(F32)
    rest = value - high
    mid = rest.astype(BF16).astype(F32)
    return high, mid, rest - mid


def gelu_slope(v):
    root = 0.7978845608028654
    t = jnp.tanh(root * (v + 0.044715 * (v * v * v)))
    return 0.5 * (1.0 + t) + 0.5 * v * (1.0 - t * t) * (root * (1.0 + 3 * 0.044715 * (v * v)))


def main_kernel(
    tok_ref, slots_ref, off_ref, cot_ref, away_ref, pick_ref, mask_ref, out_ref,
    wide, lines, packed, letters, mail, own, right_out, left_out, edge_right, edge_left,
    spill, weight, gain_pair, gath_a, gath_b, cot, norm, scaled,
    part, part_in, sums, sums_in, grads,
    acc, result, block_out, gain_own, gain_left, gain_right, gain_tiles, gain_rows, gain_mine, gain_z, gain_y, gain_out,
    mail_s, mail_r, edge_s, edge_r, core_s, core_r, one_s, one_r, two_s, two_r,
    half_s, half_r, sum_s, sum_r, pg_s, pg_r, pgc_s, pgc_r, last_s, last_r, direct_s, direct_r, res_s, res_r,
    gty_s, gty_r, gtz_s, gtz_r, gz_s, gz_r, gy_s, gy_r, gf_s, gf_r,
):
    x = lax.axis_index("dp")
    f = lax.axis_index("fsdp")
    c = f % 2
    y = (f // 2) % 8
    z = f // 16
    g = 2 * x + c
    other = 1 - c
    su = 2 + 14 * c
    sv = 16 - 14 * c
    pu = y + c * (z - y)
    pv = z + c * (y - z)
    sends = []

    def at(xx, ff):
        return {"dp": xx, "fsdp": ff}

    def mate(gg):
        return at(gg // 2, f - c + gg % 2)

    def dev_u(d):
        return at(x, ((pu + d + 8) % 8) * su + pv * sv + c)

    def dev_v(d):
        return at(x, pu * su + ((pv + d + 8) % 8) * sv + c)

    def dev_y(d):
        return at(x, z * 16 + ((y + d) % 8) * 2 + c)

    def dev_z(d):
        return at(x, ((z + d) % 8) * 16 + y * 2 + c)

    def dev_x(d):
        return at((x + d + 4) % 4, f)

    core = at(x, f - c + other)
    right = at(x, (f + 1) % 128)
    left = at(x, (f + 127) % 128)

    def copy(src, dst, ssem, rsem, dev):
        return pltpu.make_async_remote_copy(
            src_ref=src, dst_ref=dst, send_sem=ssem, recv_sem=rsem,
            device_id=dev, device_id_type=pl.DeviceIdType.MESH,
        )

    def send(src, dst, ssem, rsem, dev):
        one = copy(src, dst, ssem, rsem, dev)
        one.start()
        sends.append(one)

    def arrive(dst, ssem, rsem):
        copy(dst, dst, ssem, rsem, core).wait_recv()

    barrier = pltpu.get_barrier_semaphore()
    peers = [mate((g + r) % 8) for r in range(1, 8)]
    peers += [dev_y(r) for r in range(1, 8)] + [dev_z(r) for r in range(1, 8)] + [right, left]
    for dev in peers:
        pl.semaphore_signal(barrier, inc=1, device_id=dev, device_id_type=pl.DeviceIdType.MESH)

    tok = tok_ref[0].astype(F32)
    mean = jnp.mean(tok, axis=-1, keepdims=True)
    centered = tok - mean
    variance = jnp.mean(centered * centered, axis=-1, keepdims=True)
    scale = lax.rsqrt(variance + EPSILON)
    lane4 = lane_iota(4)
    extra = jnp.zeros((4, LANES), F32)
    for n, term in enumerate(three_terms(mean) + three_terms(scale)):
        extra = jnp.where((lane4 == n) | (lane4 == n + 8), term, extra)
    for b in range(8):
        for k in range(6):
            col = (6 * b + k) * LANES
            packed[32 * b + 4 * k : 32 * b + 4 * k + 4, :] = tok[:, col : col + LANES]
        packed[32 * b + 24 : 32 * b + 28, :] = extra
        packed[32 * b + 28 : 32 * b + 32, :] = jnp.zeros((4, LANES), F32)
    for b in range(8):
        letters[b] = packed[32 * b : 32 * b + 32, :].astype(BF16)

    pl.semaphore_wait(barrier, len(peers))
    for r in range(1, 8):
        gg = (g + r) % 8
        send(letters.at[gg], mail.at[g], mail_s.at[r - 1], mail_r.at[r - 1], mate(gg))
    mail[pl.ds(g, 1)] = letters[pl.ds(g, 1)]

    start = off_ref[f]
    length = off_ref[f + 1] - start
    shift_own = f * SHARD - start
    shift_right = shift_own + SHARD
    shift_left = shift_own - SHARD

    line16 = lax.broadcasted_iota(jnp.int32, (16, LANES), 0) * LANES + lane_iota(16)

    def widen(i, carry):
        rows = pl.ds(pl.multiple_of(i * 16, 16), 16)
        valid = line16 < length - i * (16 * LANES)
        wide[pl.ds(pl.multiple_of(FRONT + i * 16, 16), 16), :] = jnp.where(valid, slots_ref[rows, :].astype(F32), 0.0)
        return carry

    wide[0:FRONT, :] = jnp.zeros((FRONT, LANES), F32)
    wide[FRONT + LINES :, :] = jnp.zeros((BACK, LANES), F32)
    lax.fori_loop(0, LINES // 16, widen, 0, unroll=8)

    def turned(first, shift, rows):
        row = FRONT + first + lax.shift_right_arithmetic(shift, 7)
        row = jnp.clip(row, 0, FRONT + LINES + BACK - rows)
        back = (LANES - (shift & (LANES - 1))) & (LANES - 1)
        return pltpu.roll(wide[pl.ds(row, rows), :], back, 1)

    def before_cut(rows, shift):
        return lane_iota(rows) < LANES - (shift & (LANES - 1))

    def line_of(shift):
        got = turned(0, shift, 8)
        return jnp.where(before_cut(1, shift), got[0:1], got[1:2])

    def move(first_row, low, high, shift):
        def one(h, carry):
            lines[pl.ds(pl.multiple_of(h * 16, 16), 16), :] = turned((first_row + h) * 48 + 12 * x, shift, 16)
            return carry

        lax.fori_loop(low, high, one, 0, unroll=8)

    def keep(piece_ref, rows, shift):
        mask = before_cut(rows, shift)
        here = lines[pl.ds(0, rows, stride=16), :]
        for k in range(12):
            after = lines[pl.ds(k + 1, rows, stride=16), :]
            piece_ref[k // 6, :, (k % 6) * LANES : (k % 6 + 1) * LANES] = jnp.where(mask, here, after).astype(BF16)
            here = after

    gain_row = jnp.broadcast_to(line_of(shift_left + HID_DEV * D - 16), (8, LANES))
    gain_left[...] = gain_row
    send(gain_left, gain_right, core_s.at[3], core_r.at[3], left)
    gain_own[...] = jnp.broadcast_to(line_of(shift_own + HID_DEV * D - 16), (8, LANES))
    lines[0:128, :] = jnp.zeros((128, LANES), F32)
    move(64, 8, 32, shift_left)
    keep(left_out, 32, shift_left)
    send(left_out, edge_left, edge_s.at[1], edge_r.at[1], left)
    move(0, 0, 25, shift_right)
    lines[400:512, :] = jnp.zeros((112, LANES), F32)
    keep(right_out, 32, shift_right)
    send(right_out, edge_right, edge_s.at[0], edge_r.at[0], right)

    for r in range(1, 8):
        arrive(mail.at[(g - r + 8) % 8], mail_s.at[r - 1], mail_r.at[r - 1])

    posts = mail[...].reshape(256, LANES)
    out_row = lax.broadcasted_iota(jnp.int32, (A_ROWS + B_ROWS, 256), 0)
    in_row = lax.broadcasted_iota(jnp.int32, (A_ROWS + B_ROWS, 256), 1)
    token = out_row & 31
    want = 32 * (token >> 2) + 4 * (out_row >> 5) + (token & 3)
    chunk = jnp.dot((want == in_row).astype(BF16), posts, preferred_element_type=F32)
    out_row = lax.broadcasted_iota(jnp.int32, (16, 256), 0) + 16
    in_row = lax.broadcasted_iota(jnp.int32, (16, 256), 1)
    want = 32 * (out_row >> 2) + 24 + (out_row & 3)
    late = jnp.dot((want == in_row).astype(BF16), posts, preferred_element_type=F32)
    lane = lane_iota(16)
    stats = jnp.where((lane >= 8) & (lane < 16), late, chunk[192:208])
    gath_a[0, 0] = chunk[0:A_ROWS].astype(BF16)
    gath_b[0, 0, 0:80, :] = chunk[A_ROWS:192].astype(BF16)
    gath_b[0, 0, 80:96, :] = stats.astype(BF16)

    for d in (1, -1, 2, -2, 3, -3, 4):
        n = SLOT[-d]
        send(gath_a.at[0, 0], gath_a.at[n, 0], one_s.at[0, n - 1], one_r.at[0, n - 1], dev_u(d))
        send(gath_b.at[0, 0], gath_b.at[0, n], one_s.at[1, n - 1], one_r.at[1, n - 1], dev_v(d))

    move(0, 0, 96, shift_own)
    keep(own, 96, shift_own)
    arrive(gain_right, core_s.at[3], core_r.at[3])
    lane8 = lane_iota(8)
    gain_row = jnp.where((lane8 >= 16) & (lane8 < 64), gain_right[...] + gain_own[...], 0.0)
    gain_pair[pl.ds(c, 1)] = gain_row[None]
    send(gain_pair.at[c], gain_pair.at[c], core_s.at[2], core_r.at[2], core)
    apart = (z - g + 8) % 8

    def unit_a(h, n):
        return gath_a.at[2 * h : 2 * h + 2, n]

    def unit_b(h, n):
        return gath_b.at[n, 2 * h : 2 * h + 2]

    streams = ((unit_a, dev_v, 1), (unit_a, dev_v, -1), (unit_b, dev_u, 1), (unit_b, dev_u, -1))

    def lands(s, h):
        for n, (unit, dev, d) in enumerate(streams):
            if s < 4 or (h < 2) == (d == 1):
                arrive(unit(h, SLOT[-d * s]), two_s.at[n, h, s - 1], two_r.at[n, h, s - 1])

    def onward(s, h):
        for n, (unit, dev, d) in enumerate(streams):
            if s > 1:
                arrive(unit(h, SLOT[-d * (s - 1)]), two_s.at[n, h, s - 2], two_r.at[n, h, s - 2])
            if s < 4 or (h < 2) == (d == 1):
                send(
                    unit(h, SLOT[-d * (s - 1)]), unit(h, SLOT[-d * s]),
                    two_s.at[n, h, s - 1], two_r.at[n, h, s - 1], dev(d),
                )

    def first_axis(n):
        arrive(gath_a.at[n, 0], one_s.at[0, n - 1], one_r.at[0, n - 1])
        arrive(gath_b.at[0, n], one_s.at[1, n - 1], one_r.at[1, n - 1])

    first_axis(1)
    onward(1, 0)
    arrive(gain_pair.at[other], core_s.at[2], core_r.at[2])
    outs = [
        copy(gain_tiles.at[y], gain_tiles.at[y], gty_s.at[r - 1], gty_r.at[r - 1], dev_y(r)) for r in range(1, 8)
    ]

    @pl.when(apart == 0)
    def _():
        rows = jnp.concatenate([gain_pair[0, 0:1], gain_pair[1, 0:1], jnp.zeros((6, LANES), F32)], axis=0)
        gain_tiles[pl.ds(y, 1)] = rows[None]
        for one in outs:
            one.start()

    first_axis(2)
    first_axis(3)
    onward(1, 1)
    first_axis(4)
    first_axis(5)
    onward(1, 2)
    first_axis(6)
    first_axis(7)
    onward(1, 3)

    arrive(edge_left, edge_s.at[1], edge_r.at[1])
    arrive(edge_right, edge_s.at[0], edge_r.at[0])
    for half in range(2):
        spill[half, 0:32, :] = own[half, 0:32, :] + edge_right[half]
        spill[half, 32:64, :] = own[half, 32:64, :]
        spill[half, 64:96, :] = own[half, 64:96, :] + edge_left[half]
    send(spill.at[other], weight.at[c], core_s.at[0], core_r.at[0], core)
    weight[pl.ds(c, 1)] = spill[pl.ds(c, 1)]
    onward(2, 0)

    def reorder(low):
        t = lax.broadcasted_iota(jnp.int32, (1, 256), 1)
        away_y, away_z = away_ref[0:1, low : low + 256], away_ref[1:2, low : low + 256]
        home = (((z + 8 + away_z) & 7) * 8 + ((y + 8 + away_y) & 7)) * 8 + (t & 7)
        nat = lax.broadcasted_iota(jnp.int32, (512, 256), 0)
        cot[:, low : low + 256] = jnp.dot(cot_ref[...], (nat == home).astype(BF16), preferred_element_type=F32)

    reorder(0)
    onward(2, 1)
    reorder(256)
    onward(2, 2)
    outs_z = [copy(gain_tiles, gain_tiles, gtz_s.at[r - 1], gtz_r, dev_z(r)) for r in range(1, 8)]

    @pl.when(apart == 0)
    def _():
        for r in range(1, 8):
            arrive(gain_tiles.at[(y - r + 8) % 8], gty_s.at[r - 1], gty_r.at[r - 1])
        for one in outs:
            one.wait_send()
        for one in outs_z:
            one.start()

    onward(2, 3)
    arrive(weight.at[other], core_s.at[0], core_r.at[0])
    onward(3, 0)
    onward(3, 1)

    @pl.when(apart != 0)
    def _():
        arrive(gain_tiles, gtz_s.at[0], gtz_r)

    @pl.when(apart == 0)
    def _():
        for one in outs_z:
            one.wait_send()

    for yy in range(8):
        gain_rows[2 * yy : 2 * yy + 2, :] = gain_tiles[yy, 0:2, :]
    spread = jnp.dot(gain_rows[...].astype(BF16), pick_ref[...], preferred_element_type=F32)
    gain = jnp.sum(spread * mask_ref[...], axis=0, keepdims=True)

    def normalize(first, places):
        data = []
        for a, b in places:
            uu, vv = a + c * (b - a), b + c * (a - b)
            rows = gath_b[uu, vv, 80:96, :].astype(F32)
            cols = []
            for base in (0, 3):
                early = (rows[:, base : base + 1] + rows[:, base + 1 : base + 2]) + rows[:, base + 2 : base + 3]
                late = (rows[:, base + 8 : base + 9] + rows[:, base + 9 : base + 10]) + rows[:, base + 10 : base + 11]
                cols.append((early[0:8], early[8:16], late[0:8], late[8:16]))
            data.append((uu, vv, cols))
        for k in range(6):
            gain_k = gain[:, k * LANES : (k + 1) * LANES]
            tiles = []
            for uu, vv, _ in data:
                if k < 3:
                    tile = gath_a[uu, vv, 32 * k : 32 * k + 32, :].astype(F32)
                elif k == 3:
                    tile = jnp.concatenate(
                        [gath_a[uu, vv, 96:112, :].astype(F32), gath_b[uu, vv, 0:16, :].astype(F32)], axis=0
                    )
                else:
                    tile = gath_b[uu, vv, 32 * k - 112 : 32 * k - 80, :].astype(F32)
                tiles.append(tile)
            for xx in range(4):
                both = jnp.concatenate(
                    [
                        (tiles[side][8 * xx : 8 * xx + 8] - data[side][2][0][xx]) * data[side][2][1][xx]
                        for side in range(2)
                    ],
                    axis=0,
                )
                rows = pl.ds(512 * xx + 8 * first, 16)
                norm[rows, k * LANES : (k + 1) * LANES] = both
                scaled[rows, k * LANES : (k + 1) * LANES] = (both * gain_k).astype(BF16)

    def pairs(n, place, low=0, high=16):
        for e in range(low, high, 2):
            normalize(16 * n + e, (place(e), place(e + 1)))

    block = weight[...].reshape(192, BLOCK)

    def rows_of(n, xx):
        return slice(512 * xx + SIZE * n, 512 * xx + SIZE * (n + 1))

    def pre_act(n):
        for xx in range(4):
            got = lax.dot_general(
                block, scaled[rows_of(n, xx), :], (((1,), (1,)), ((), ())), preferred_element_type=F32
            )
            part[n, 0, xx] = got[0:96]
            part[n, 1, xx] = got[96:192]
        send(part.at[n, other], part_in.at[n], half_s.at[n], half_r.at[n], core)

    def sum_x(n):
        arrive(part_in.at[n], half_s.at[n], half_r.at[n])
        sums[n] = part[n, pl.ds(c, 1)][0] + part_in[n]
        for r in range(1, 4):
            send(sums.at[n, (x + r) % 4], sums_in.at[n, r - 1], sum_s.at[n, r - 1], sum_r.at[n, r - 1], dev_x(r))

    def last_pre_act(n):
        for r in (2, 1, 3, 0):
            xx = (x + r) % 4
            rows = scaled[pl.ds(pl.multiple_of(512 * xx + SIZE * n, SIZE), SIZE), :]
            got = lax.dot_general(block, rows, (((1,), (1,)), ((), ())), preferred_element_type=F32)
            part[n, 0, pl.ds(xx, 1)] = got[0:96][None]
            part[n, 1, pl.ds(xx, 1)] = got[96:192][None]
            send(part.at[n, other, xx], part_in.at[n, xx], last_s.at[r], last_r.at[r], core)

    def last_sum_x(n):
        for r in (2, 1, 3, 0):
            xx = (x + r) % 4
            arrive(part_in.at[n, xx], last_s.at[r], last_r.at[r])
            sums[n, pl.ds(xx, 1)] = part[n, pl.ds(c, 1), pl.ds(xx, 1)][0] + part_in[n, pl.ds(xx, 1)]
            if r:
                send(sums.at[n, xx], sums_in.at[n, r - 1], sum_s.at[n, r - 1], sum_r.at[n, r - 1], dev_x(r))

    mine = pl.ds(pl.multiple_of(96 * c, 32), 96)
    theirs = pl.ds(pl.multiple_of(96 * other, 32), 96)

    def slope(n):
        for r in range(1, 4):
            arrive(sums_in.at[n, r - 1], sum_s.at[n, r - 1], sum_r.at[n, r - 1])
        total = (sums[n, pl.ds(x, 1)][0] + sums_in[n, 0]) + (sums_in[n, 1] + sums_in[n, 2])
        got = (cot[:, SIZE * n : SIZE * (n + 1)] * gelu_slope(total)).astype(BF16)
        grads[n, pl.ds(x, 1), mine, :] = got[None]
        if n == SETS - 1:
            for r in (4, 5, 3, 2, 6, 1, 7):
                send(grads.at[n, x, mine], grads.at[n, x, mine], direct_s.at[r - 1], direct_r.at[r - 1], mate((g + r) % 8))
        else:
            for r in range(1, 4):
                send(grads.at[n, x, mine], grads.at[n, x, mine], pg_s.at[n, r - 1], pg_r.at[n, r - 1], dev_x(r))

    def last_shared(n):
        for r in range(1, 8):
            gg = (g - r + 8) % 8
            rows = pl.ds(pl.multiple_of(96 * (gg % 2), 32), 96)
            arrive(grads.at[n, gg // 2, rows], direct_s.at[r - 1], direct_r.at[r - 1])

    def share(n):
        for r in range(1, 4):
            arrive(grads.at[n, (x - r + 4) % 4, mine], pg_s.at[n, r - 1], pg_r.at[n, r - 1])
        send(grads.at[n, :, mine], grads.at[n, :, mine], pgc_s.at[n], pgc_r.at[n], core)

    def shared(n):
        arrive(grads.at[n, :, theirs], pgc_s.at[n], pgc_r.at[n])

    def gradient(n):
        total = jnp.zeros((192, BLOCK), F32)
        for xx in range(4):
            total += jnp.dot(grads[n, xx], scaled[rows_of(n, xx), :], preferred_element_type=F32)
        return total

    def gain_part(n):
        total = jnp.zeros((1, BLOCK), F32)
        for xx in range(4):
            back = lax.dot_general(grads[n, xx], block, (((0,), (0,)), ((), ())), preferred_element_type=F32)
            total += jnp.sum(back * norm[rows_of(n, xx), :], axis=0, keepdims=True)
        return total

    pairs(0, near)
    pre_act(0)
    onward(3, 2)
    sum_x(0)
    onward(3, 3)
    onward(4, 0)
    onward(4, 1)
    pairs(1, side)
    pre_act(1)
    onward(4, 2)
    sum_x(1)
    pairs(2, corner, 0, 8)
    onward(4, 3)
    pairs(2, corner, 8, 16)
    pre_act(2)
    sum_x(2)
    slope(0)
    for h in range(4):
        lands(4, h)
    pairs(3, far)
    last_pre_act(3)
    last_sum_x(3)
    slope(1)
    share(0)
    shared(0)
    acc[...] = gradient(0)
    gain_sum = gain_part(0)
    slope(2)
    share(1)
    early = list(sends)
    sends.clear()
    slope(3)
    shared(1)
    acc[...] += gradient(1)
    gain_sum += gain_part(1)
    share(2)
    shared(2)
    acc[...] += gradient(2)
    gain_sum += gain_part(2)
    for one in early:
        one.wait_send()
    last_shared(3)
    gain_sum += gain_part(3)
    for k in range(6):
        gain_mine[k : k + 1, :] = gain_sum[:, k * LANES : (k + 1) * LANES]
    gain_mine[6:8, :] = jnp.zeros((2, LANES), F32)

    to_z = copy(gain_mine, gain_z.at[(apart + 7) % 8], gz_s, gz_r.at[(apart + 7) % 8], at(x, g * 16 + y * 2 + c))

    @pl.when(apart != 0)
    def _():
        to_z.start()

    rounded = (acc[...] + gradient(3)).astype(BF16)

    block_out[0] = rounded[0:96]
    block_out[1] = rounded[96:192]
    send(block_out.at[other], result.at[x, c], core_s.at[1], core_r.at[1], core)
    result[pl.ds(x, 1), pl.ds(c, 1)] = block_out[pl.ds(c, 1)][None]
    way = 1 - 2 * c
    send(result.at[x, c], result.at[x, c], res_s.at[c, 0], res_r.at[c, 0], dev_x(way))
    arrive(result.at[x, other], core_s.at[1], core_r.at[1])
    send(result.at[x, other], result.at[x, other], res_s.at[other, 0], res_r.at[other, 0], dev_x(-way))
    send(result.at[x, other], result.at[x, other], res_s.at[c, 1], res_r.at[c, 1], dev_x(way))
    send(result.at[x, c], result.at[x, c], res_s.at[other, 1], res_r.at[other, 1], dev_x(-way))

    def spell(xx, half):
        for k in range(6):
            col = result[xx, half, :, k * LANES : (k + 1) * LANES].astype(F32)
            out_ref[pl.ds(12 * xx + 6 * half + k, 96, stride=48), :] = col

    for half in range(2):
        spell(x, half)

    outs_y = [copy(gain_y.at[7], gain_y.at[r - 1], gy_s.at[r - 1], gy_r.at[r - 1], dev_y(r)) for r in range(1, 8)]

    @pl.when(apart == 0)
    def _():
        sum_z = gain_mine[...]
        for r in range(7):
            arrive(gain_z.at[r], gz_s, gz_r.at[r])
            sum_z += gain_z[r]
        gain_y[7] = sum_z
        for one in outs_y:
            one.start()

    for m, d in enumerate((1, -1)):
        arrive(result.at[(x - d + 4) % 4, m], res_s.at[m, 0], res_r.at[m, 0])
        send(result.at[(x - d + 4) % 4, m], result.at[(x - d + 4) % 4, m], res_s.at[m, 2], res_r.at[m, 2], dev_x(d))

    outs_f = [copy(gain_out, gain_out, gf_s.at[r - 1], gf_r, mate((g + r) % 8)) for r in range(1, 8)]

    @pl.when(apart == 0)
    def _():
        sum_y = gain_y[7]
        for r in range(7):
            arrive(gain_y.at[r], gy_s.at[r], gy_r.at[r])
            sum_y += gain_y[r]
        gain_out[...] = sum_y
        for one in outs_f:
            one.start()

    for m, d in enumerate((1, -1)):
        spell((x - d + 4) % 4, m)
    for m, d in enumerate((1, -1)):
        arrive(result.at[(x - d + 4) % 4, 1 - m], res_s.at[m, 1], res_r.at[m, 1])
        spell((x - d + 4) % 4, 1 - m)

    @pl.when(apart != 0)
    def _():
        arrive(gain_out, gf_s.at[0], gf_r)
        to_z.wait_send()

    @pl.when(apart == 0)
    def _():
        for one in outs_y:
            one.wait_send()
        for one in outs_f:
            one.wait_send()

    first = 48 * (2 * y + c)
    turn = first % LANES
    line = first // LANES
    here = jnp.broadcast_to(gain_out[pl.ds(line, 1), :], (8, LANES))
    after = jnp.broadcast_to(gain_out[pl.ds(line + 1, 1), :], (8, LANES))
    back = (LANES - turn) % LANES
    moved = jnp.where(lane_iota(8) < LANES - turn, pltpu.roll(here, back, 1), pltpu.roll(after, back, 1))
    out_ref[4608:4616, :] = moved

    arrive(result.at[(x + 2) % 4, 0], res_s.at[0, 2], res_r.at[0, 2])
    spell((x + 2) % 4, 0)
    arrive(result.at[(x + 2) % 4, 1], res_s.at[1, 2], res_r.at[1, 2])
    spell((x + 2) % 4, 1)
    for one in sends:
        one.wait_send()


def body(tokens, act_cot, old_slots, offsets):
    vmem = pl.BlockSpec(memory_space=pltpu.VMEM)
    smem = pl.BlockSpec(memory_space=pltpu.SMEM)
    dma = pltpu.SemaphoreType.DMA
    slots = jnp.pad(old_slots, (0, LINES * LANES - old_slots.shape[0])).reshape(LINES, LANES)
    chips = chips_in_order()
    away = np.array([[AWAY[chip[axis]] for chip in chips for _ in range(8)] for axis in range(2)], np.int32)
    n = np.arange(BLOCK)
    lanes = np.arange(LANES)[:, None]
    pick = jnp.asarray((lanes == 16 + n % 48).astype(np.float32), BF16)
    mask = jnp.asarray((np.arange(16)[:, None] == n // 48).astype(np.float32))
    out = pl.pallas_call(
        main_kernel,
        out_shape=jax.ShapeDtypeStruct((4616, LANES), F32),
        in_specs=[vmem, vmem, smem, vmem, vmem, vmem, vmem],
        out_specs=vmem,
        scratch_shapes=[
            pltpu.VMEM((FRONT + LINES + BACK, LANES), F32),
            pltpu.VMEM((96 * 16, LANES), F32),
            pltpu.VMEM((256, LANES), F32),
            pltpu.VMEM((8, 32, LANES), BF16),
            pltpu.VMEM((8, 32, LANES), BF16),
            pltpu.VMEM((2, 96, BLOCK), BF16),
            pltpu.VMEM((2, 32, BLOCK), BF16),
            pltpu.VMEM((2, 32, BLOCK), BF16),
            pltpu.VMEM((2, 32, BLOCK), BF16),
            pltpu.VMEM((2, 32, BLOCK), BF16),
            pltpu.VMEM((2, 96, BLOCK), BF16),
            pltpu.VMEM((2, 96, BLOCK), BF16),
            pltpu.VMEM((2, 8, LANES), F32),
            pltpu.VMEM((8, 8, A_ROWS, LANES), BF16),
            pltpu.VMEM((8, 8, B_ROWS, LANES), BF16),
            pltpu.VMEM((96, 512), F32),
            pltpu.VMEM((2048, BLOCK), F32),
            pltpu.VMEM((2048, BLOCK), BF16),
            pltpu.VMEM((SETS, 2, 4, 96, SIZE), F32),
            pltpu.VMEM((SETS, 4, 96, SIZE), F32),
            pltpu.VMEM((SETS, 4, 96, SIZE), F32),
            pltpu.VMEM((SETS, 3, 96, SIZE), F32),
            pltpu.VMEM((SETS, 4, 192, SIZE), BF16),
            pltpu.VMEM((192, BLOCK), F32),
            pltpu.VMEM((4, 2, 96, BLOCK), BF16),
            pltpu.VMEM((2, 96, BLOCK), BF16),
            pltpu.VMEM((8, LANES), F32),
            pltpu.VMEM((8, LANES), F32),
            pltpu.VMEM((8, LANES), F32),
            pltpu.VMEM((8, 8, LANES), F32),
            pltpu.VMEM((16, LANES), F32),
            pltpu.VMEM((8, LANES), F32),
            pltpu.VMEM((8, 8, LANES), F32),
            pltpu.VMEM((8, 8, LANES), F32),
            pltpu.VMEM((8, LANES), F32),
            dma((7,)), dma((7,)),
            dma((2,)), dma((2,)),
            dma((4,)), dma((4,)),
            dma((2, 7)), dma((2, 7)),
            dma((4, 4, 4)), dma((4, 4, 4)),
            dma((SETS,)), dma((SETS,)),
            dma((SETS, 3)), dma((SETS, 3)),
            dma((SETS, 3)), dma((SETS, 3)),
            dma((SETS,)), dma((SETS,)),
            dma((4,)), dma((4,)),
            dma((7,)), dma((7,)),
            dma((2, 3)), dma((2, 3)),
            dma((7,)), dma((7,)),
            dma((7,)), dma,
            dma, dma((8,)),
            dma((7,)), dma((7,)),
            dma((7,)), dma,
        ],
        compiler_params=pltpu.CompilerParams(
            collective_id=0, has_side_effects=True, vmem_limit_bytes=40 * 2**20
        ),
    )(tokens, slots, offsets, act_cot[0].T, jnp.asarray(away), pick, mask)
    return out.reshape(-1)[:SHARD]


def solution(mesh):
    placed = (P("dp", "fsdp", None), P("dp", None, "fsdp"), P("fsdp"), P())
    return jax.shard_map(body, mesh=mesh, in_specs=placed, out_specs=P("fsdp"), check_vma=False)
```

```python
import jax
import jax.numpy as jnp
import numpy as np
from jax import lax
from jax.experimental import pallas as pl
from jax.experimental.pallas import tpu as pltpu
from jax.sharding import PartitionSpec as P

D = 6144
HID_DEV = 96
SHARD = 589872
EPSILON = 1e-06
LINES = 6928
FRONT = 2320
BACK = 64
BLOCK = 768
LANES = 128
A_ROWS = 112
B_ROWS = 96
F32 = jnp.float32
BF16 = jnp.bfloat16
AWAY = (0, 1, -1, 2, -2, 3, -3, 4)
SLOT = {d: n for n, d in enumerate(AWAY)}
SLOT[-4] = SLOT[4]
SETS = 4
SIZE = 128


def chips_in_order():
    return [place(e) for place in (near, side, corner, far) for e in range(16)]


def near(e):
    return e % 4, e // 4


def side(e):
    beyond = e // 12
    return (1 - beyond) * (4 + e % 3) + beyond * (e - 12), (1 - beyond) * (e // 3) + beyond * 4


def corner(e):
    beyond = e // 8
    return (1 - beyond) * (e % 4) + beyond * (4 + (e - 8) % 3), (1 - beyond) * (5 + e // 4) + beyond * (4 + (e - 8) // 3)


def far(e):
    beyond = e // 8
    last = e // 15
    return (1 - beyond) * e + beyond * (7 - last), (1 - beyond) * 7 + beyond * (e - 8 - last)


def lane_iota(rows):
    return lax.broadcasted_iota(jnp.int32, (rows, LANES), 1)


def three_terms(value):
    high = value.astype(BF16).astype(F32)
    rest = value - high
    mid = rest.astype(BF16).astype(F32)
    return high, mid, rest - mid


def gelu_slope(v):
    root = 0.7978845608028654
    t = jnp.tanh(root * (v + 0.044715 * (v * v * v)))
    return 0.5 * (1.0 + t) + 0.5 * v * (1.0 - t * t) * (root * (1.0 + 3 * 0.044715 * (v * v)))


def main_kernel(
    tok_ref, slots_ref, off_ref, cot_ref, away_ref, pick_ref, mask_ref, out_ref,
    wide, lines, packed, letters, mail, own, right_out, left_out, edge_right, edge_left,
    spill, weight, gain_pair, gath_a, gath_b, cot, norm, scaled,
    part, part_in, sums, sums_in, grads,
    acc, result, block_out, gain_own, gain_left, gain_right, gain_tiles, gain_rows, gain_mine, gain_z, gain_y, gain_out,
    mail_s, mail_r, edge_s, edge_r, core_s, core_r, one_s, one_r, two_s, two_r,
    half_s, half_r, sum_s, sum_r, pg_s, pg_r, pgc_s, pgc_r, last_s, last_r, direct_s, direct_r, res_s, res_r,
    gty_s, gty_r, gtz_s, gtz_r, gz_s, gz_r, gy_s, gy_r, gf_s, gf_r,
):
    x = lax.axis_index("dp")
    f = lax.axis_index("fsdp")
    c = f % 2
    y = (f // 2) % 8
    z = f // 16
    g = 2 * x + c
    other = 1 - c
    su = 2 + 14 * c
    sv = 16 - 14 * c
    pu = y + c * (z - y)
    pv = z + c * (y - z)
    sends = []

    def at(xx, ff):
        return {"dp": xx, "fsdp": ff}

    def mate(gg):
        return at(gg // 2, f - c + gg % 2)

    def dev_u(d):
        return at(x, ((pu + d + 8) % 8) * su + pv * sv + c)

    def dev_v(d):
        return at(x, pu * su + ((pv + d + 8) % 8) * sv + c)

    def dev_y(d):
        return at(x, z * 16 + ((y + d) % 8) * 2 + c)

    def dev_z(d):
        return at(x, ((z + d) % 8) * 16 + y * 2 + c)

    def dev_x(d):
        return at((x + d + 4) % 4, f)

    core = at(x, f - c + other)
    right = at(x, (f + 1) % 128)
    left = at(x, (f + 127) % 128)

    def copy(src, dst, ssem, rsem, dev):
        return pltpu.make_async_remote_copy(
            src_ref=src, dst_ref=dst, send_sem=ssem, recv_sem=rsem,
            device_id=dev, device_id_type=pl.DeviceIdType.MESH,
        )

    def send(src, dst, ssem, rsem, dev):
        one = copy(src, dst, ssem, rsem, dev)
        one.start()
        sends.append(one)

    def arrive(dst, ssem, rsem):
        copy(dst, dst, ssem, rsem, core).wait_recv()

    barrier = pltpu.get_barrier_semaphore()
    peers = [mate((g + r) % 8) for r in range(1, 8)]
    peers += [dev_y(r) for r in range(1, 8)] + [dev_z(r) for r in range(1, 8)] + [right, left]
    for dev in peers:
        pl.semaphore_signal(barrier, inc=1, device_id=dev, device_id_type=pl.DeviceIdType.MESH)

    tok = tok_ref[0].astype(F32)
    mean = jnp.mean(tok, axis=-1, keepdims=True)
    centered = tok - mean
    variance = jnp.mean(centered * centered, axis=-1, keepdims=True)
    scale = lax.rsqrt(variance + EPSILON)
    lane4 = lane_iota(4)
    extra = jnp.zeros((4, LANES), F32)
    for n, term in enumerate(three_terms(mean) + three_terms(scale)):
        extra = jnp.where((lane4 == n) | (lane4 == n + 8), term, extra)
    for b in range(8):
        for k in range(6):
            col = (6 * b + k) * LANES
            packed[32 * b + 4 * k : 32 * b + 4 * k + 4, :] = tok[:, col : col + LANES]
        packed[32 * b + 24 : 32 * b + 28, :] = extra
        packed[32 * b + 28 : 32 * b + 32, :] = jnp.zeros((4, LANES), F32)
    for b in range(8):
        letters[b] = packed[32 * b : 32 * b + 32, :].astype(BF16)

    pl.semaphore_wait(barrier, len(peers))
    for r in range(1, 8):
        gg = (g + r) % 8
        send(letters.at[gg], mail.at[g], mail_s.at[r - 1], mail_r.at[r - 1], mate(gg))
    mail[pl.ds(g, 1)] = letters[pl.ds(g, 1)]

    start = off_ref[f]
    length = off_ref[f + 1] - start
    shift_own = f * SHARD - start
    shift_right = shift_own + SHARD
    shift_left = shift_own - SHARD

    line16 = lax.broadcasted_iota(jnp.int32, (16, LANES), 0) * LANES + lane_iota(16)

    def widen(i, carry):
        rows = pl.ds(pl.multiple_of(i * 16, 16), 16)
        valid = line16 < length - i * (16 * LANES)
        wide[pl.ds(pl.multiple_of(FRONT + i * 16, 16), 16), :] = jnp.where(valid, slots_ref[rows, :].astype(F32), 0.0)
        return carry

    wide[0:FRONT, :] = jnp.zeros((FRONT, LANES), F32)
    wide[FRONT + LINES :, :] = jnp.zeros((BACK, LANES), F32)
    lax.fori_loop(0, LINES // 16, widen, 0, unroll=8)

    def turned(first, shift, rows):
        row = FRONT + first + lax.shift_right_arithmetic(shift, 7)
        row = jnp.clip(row, 0, FRONT + LINES + BACK - rows)
        back = (LANES - (shift & (LANES - 1))) & (LANES - 1)
        return pltpu.roll(wide[pl.ds(row, rows), :], back, 1)

    def before_cut(rows, shift):
        return lane_iota(rows) < LANES - (shift & (LANES - 1))

    def line_of(shift):
        got = turned(0, shift, 8)
        return jnp.where(before_cut(1, shift), got[0:1], got[1:2])

    def move(first_row, low, high, shift):
        def one(h, carry):
            lines[pl.ds(pl.multiple_of(h * 16, 16), 16), :] = turned((first_row + h) * 48 + 12 * x, shift, 16)
            return carry

        lax.fori_loop(low, high, one, 0, unroll=8)

    def keep(piece_ref, rows, shift):
        mask = before_cut(rows, shift)
        here = lines[pl.ds(0, rows, stride=16), :]
        for k in range(12):
            after = lines[pl.ds(k + 1, rows, stride=16), :]
            piece_ref[k // 6, :, (k % 6) * LANES : (k % 6 + 1) * LANES] = jnp.where(mask, here, after).astype(BF16)
            here = after

    gain_row = jnp.broadcast_to(line_of(shift_left + HID_DEV * D - 16), (8, LANES))
    gain_left[...] = gain_row
    send(gain_left, gain_right, core_s.at[3], core_r.at[3], left)
    gain_own[...] = jnp.broadcast_to(line_of(shift_own + HID_DEV * D - 16), (8, LANES))
    lines[0:128, :] = jnp.zeros((128, LANES), F32)
    move(64, 8, 32, shift_left)
    keep(left_out, 32, shift_left)
    send(left_out, edge_left, edge_s.at[1], edge_r.at[1], left)
    move(0, 0, 25, shift_right)
    lines[400:512, :] = jnp.zeros((112, LANES), F32)
    keep(right_out, 32, shift_right)
    send(right_out, edge_right, edge_s.at[0], edge_r.at[0], right)

    for r in range(1, 8):
        arrive(mail.at[(g - r + 8) % 8], mail_s.at[r - 1], mail_r.at[r - 1])

    posts = mail[...].reshape(256, LANES)
    out_row = lax.broadcasted_iota(jnp.int32, (A_ROWS + B_ROWS, 256), 0)
    in_row = lax.broadcasted_iota(jnp.int32, (A_ROWS + B_ROWS, 256), 1)
    token = out_row & 31
    want = 32 * (token >> 2) + 4 * (out_row >> 5) + (token & 3)
    chunk = jnp.dot((want == in_row).astype(BF16), posts, preferred_element_type=F32)
    out_row = lax.broadcasted_iota(jnp.int32, (16, 256), 0) + 16
    in_row = lax.broadcasted_iota(jnp.int32, (16, 256), 1)
    want = 32 * (out_row >> 2) + 24 + (out_row & 3)
    late = jnp.dot((want == in_row).astype(BF16), posts, preferred_element_type=F32)
    lane = lane_iota(16)
    stats = jnp.where((lane >= 8) & (lane < 16), late, chunk[192:208])
    gath_a[0, 0] = chunk[0:A_ROWS].astype(BF16)
    gath_b[0, 0, 0:80, :] = chunk[A_ROWS:192].astype(BF16)
    gath_b[0, 0, 80:96, :] = stats.astype(BF16)

    for d in (1, -1, 2, -2, 3, -3, 4):
        n = SLOT[-d]
        send(gath_a.at[0, 0], gath_a.at[n, 0], one_s.at[0, n - 1], one_r.at[0, n - 1], dev_u(d))
        send(gath_b.at[0, 0], gath_b.at[0, n], one_s.at[1, n - 1], one_r.at[1, n - 1], dev_v(d))

    move(0, 0, 96, shift_own)
    keep(own, 96, shift_own)
    arrive(gain_right, core_s.at[3], core_r.at[3])
    lane8 = lane_iota(8)
    gain_row = jnp.where((lane8 >= 16) & (lane8 < 64), gain_right[...] + gain_own[...], 0.0)
    gain_pair[pl.ds(c, 1)] = gain_row[None]
    send(gain_pair.at[c], gain_pair.at[c], core_s.at[2], core_r.at[2], core)
    apart = (z - g + 8) % 8

    def unit_a(h, n):
        return gath_a.at[2 * h : 2 * h + 2, n]

    def unit_b(h, n):
        return gath_b.at[n, 2 * h : 2 * h + 2]

    streams = ((unit_a, dev_v, 1), (unit_a, dev_v, -1), (unit_b, dev_u, 1), (unit_b, dev_u, -1))

    def lands(s, h):
        for n, (unit, dev, d) in enumerate(streams):
            if s < 4 or (h < 2) == (d == 1):
                arrive(unit(h, SLOT[-d * s]), two_s.at[n, h, s - 1], two_r.at[n, h, s - 1])

    def onward(s, h):
        if s > 1:
            lands(s - 1, h)
        for n, (unit, dev, d) in enumerate(streams):
            if s < 4 or (h < 2) == (d == 1):
                send(
                    unit(h, SLOT[-d * (s - 1)]), unit(h, SLOT[-d * s]),
                    two_s.at[n, h, s - 1], two_r.at[n, h, s - 1], dev(d),
                )

    def first_axis(n):
        arrive(gath_a.at[n, 0], one_s.at[0, n - 1], one_r.at[0, n - 1])
        arrive(gath_b.at[0, n], one_s.at[1, n - 1], one_r.at[1, n - 1])

    first_axis(1)
    onward(1, 0)
    arrive(gain_pair.at[other], core_s.at[2], core_r.at[2])
    outs = [
        copy(gain_tiles.at[y], gain_tiles.at[y], gty_s.at[r - 1], gty_r.at[r - 1], dev_y(r)) for r in range(1, 8)
    ]

    @pl.when(apart == 0)
    def _():
        rows = jnp.concatenate([gain_pair[0, 0:1], gain_pair[1, 0:1], jnp.zeros((6, LANES), F32)], axis=0)
        gain_tiles[pl.ds(y, 1)] = rows[None]
        for one in outs:
            one.start()

    first_axis(2)
    first_axis(3)
    onward(1, 1)
    first_axis(4)
    first_axis(5)
    onward(1, 2)
    first_axis(6)
    first_axis(7)
    onward(1, 3)

    arrive(edge_left, edge_s.at[1], edge_r.at[1])
    arrive(edge_right, edge_s.at[0], edge_r.at[0])
    for half in range(2):
        spill[half, 0:32, :] = own[half, 0:32, :] + edge_right[half]
        spill[half, 32:64, :] = own[half, 32:64, :]
        spill[half, 64:96, :] = own[half, 64:96, :] + edge_left[half]
    send(spill.at[other], weight.at[c], core_s.at[0], core_r.at[0], core)
    weight[pl.ds(c, 1)] = spill[pl.ds(c, 1)]
    onward(2, 0)

    def reorder(low):
        t = lax.broadcasted_iota(jnp.int32, (1, 256), 1)
        away_y, away_z = away_ref[0:1, low : low + 256], away_ref[1:2, low : low + 256]
        home = (((z + 8 + away_z) & 7) * 8 + ((y + 8 + away_y) & 7)) * 8 + (t & 7)
        nat = lax.broadcasted_iota(jnp.int32, (512, 256), 0)
        cot[:, low : low + 256] = jnp.dot(cot_ref[...], (nat == home).astype(BF16), preferred_element_type=F32)

    reorder(0)
    onward(2, 1)
    reorder(256)
    onward(2, 2)
    outs_z = [copy(gain_tiles, gain_tiles, gtz_s.at[r - 1], gtz_r, dev_z(r)) for r in range(1, 8)]

    @pl.when(apart == 0)
    def _():
        for r in range(1, 8):
            arrive(gain_tiles.at[(y - r + 8) % 8], gty_s.at[r - 1], gty_r.at[r - 1])
        for one in outs:
            one.wait_send()
        for one in outs_z:
            one.start()

    onward(2, 3)
    arrive(weight.at[other], core_s.at[0], core_r.at[0])
    onward(3, 0)
    onward(3, 1)

    @pl.when(apart != 0)
    def _():
        arrive(gain_tiles, gtz_s.at[0], gtz_r)

    @pl.when(apart == 0)
    def _():
        for one in outs_z:
            one.wait_send()

    for yy in range(8):
        gain_rows[2 * yy : 2 * yy + 2, :] = gain_tiles[yy, 0:2, :]
    spread = jnp.dot(gain_rows[...].astype(BF16), pick_ref[...], preferred_element_type=F32)
    gain = jnp.sum(spread * mask_ref[...], axis=0, keepdims=True)

    def normalize(first, places):
        data = []
        for a, b in places:
            uu, vv = a + c * (b - a), b + c * (a - b)
            rows = gath_b[uu, vv, 80:96, :].astype(F32)
            cols = []
            for base in (0, 3):
                early = (rows[:, base : base + 1] + rows[:, base + 1 : base + 2]) + rows[:, base + 2 : base + 3]
                late = (rows[:, base + 8 : base + 9] + rows[:, base + 9 : base + 10]) + rows[:, base + 10 : base + 11]
                cols.append((early[0:8], early[8:16], late[0:8], late[8:16]))
            data.append((uu, vv, cols))
        for k in range(6):
            gain_k = gain[:, k * LANES : (k + 1) * LANES]
            tiles = []
            for uu, vv, _ in data:
                if k < 3:
                    tile = gath_a[uu, vv, 32 * k : 32 * k + 32, :].astype(F32)
                elif k == 3:
                    tile = jnp.concatenate(
                        [gath_a[uu, vv, 96:112, :].astype(F32), gath_b[uu, vv, 0:16, :].astype(F32)], axis=0
                    )
                else:
                    tile = gath_b[uu, vv, 32 * k - 112 : 32 * k - 80, :].astype(F32)
                tiles.append(tile)
            for xx in range(4):
                both = jnp.concatenate(
                    [
                        (tiles[side][8 * xx : 8 * xx + 8] - data[side][2][0][xx]) * data[side][2][1][xx]
                        for side in range(2)
                    ],
                    axis=0,
                )
                rows = pl.ds(512 * xx + 8 * first, 16)
                norm[rows, k * LANES : (k + 1) * LANES] = both
                scaled[rows, k * LANES : (k + 1) * LANES] = (both * gain_k).astype(BF16)

    def pairs(n, place, low=0, high=16):
        for e in range(low, high, 2):
            normalize(16 * n + e, (place(e), place(e + 1)))

    block = weight[...].reshape(192, BLOCK)

    def rows_of(n, xx):
        return slice(512 * xx + SIZE * n, 512 * xx + SIZE * (n + 1))

    def pre_act(n):
        for xx in range(4):
            got = lax.dot_general(
                block, scaled[rows_of(n, xx), :], (((1,), (1,)), ((), ())), preferred_element_type=F32
            )
            part[n, 0, xx] = got[0:96]
            part[n, 1, xx] = got[96:192]
        send(part.at[n, other], part_in.at[n], half_s.at[n], half_r.at[n], core)

    def sum_x(n):
        arrive(part_in.at[n], half_s.at[n], half_r.at[n])
        sums[n] = part[n, pl.ds(c, 1)][0] + part_in[n]
        for r in (2, 1, 3):
            send(sums.at[n, (x + r) % 4], sums_in.at[n, r - 1], sum_s.at[n, r - 1], sum_r.at[n, r - 1], dev_x(r))

    def last_pre_act(n):
        for r in (2, 1, 3, 0):
            xx = (x + r) % 4
            rows = scaled[pl.ds(pl.multiple_of(512 * xx + SIZE * n, SIZE), SIZE), :]
            got = lax.dot_general(block, rows, (((1,), (1,)), ((), ())), preferred_element_type=F32)
            part[n, 0, pl.ds(xx, 1)] = got[0:96][None]
            part[n, 1, pl.ds(xx, 1)] = got[96:192][None]
            send(part.at[n, other, xx], part_in.at[n, xx], last_s.at[r], last_r.at[r], core)

    def last_sum_x(n):
        for r in (2, 1, 3, 0):
            xx = (x + r) % 4
            arrive(part_in.at[n, xx], last_s.at[r], last_r.at[r])
            sums[n, pl.ds(xx, 1)] = part[n, pl.ds(c, 1), pl.ds(xx, 1)][0] + part_in[n, pl.ds(xx, 1)]
            if r:
                send(sums.at[n, xx], sums_in.at[n, r - 1], sum_s.at[n, r - 1], sum_r.at[n, r - 1], dev_x(r))

    mine = pl.ds(pl.multiple_of(96 * c, 32), 96)
    theirs = pl.ds(pl.multiple_of(96 * other, 32), 96)

    def slope(n):
        for r in range(1, 4):
            arrive(sums_in.at[n, r - 1], sum_s.at[n, r - 1], sum_r.at[n, r - 1])
        total = (sums[n, pl.ds(x, 1)][0] + sums_in[n, 0]) + (sums_in[n, 1] + sums_in[n, 2])
        got = (cot[:, SIZE * n : SIZE * (n + 1)] * gelu_slope(total)).astype(BF16)
        grads[n, pl.ds(x, 1), mine, :] = got[None]
        if n == SETS - 1:
            for r in (4, 5, 3, 2, 6, 1, 7):
                send(grads.at[n, x, mine], grads.at[n, x, mine], direct_s.at[r - 1], direct_r.at[r - 1], mate((g + r) % 8))
        else:
            for r in (2, 1, 3):
                send(grads.at[n, x, mine], grads.at[n, x, mine], pg_s.at[n, r - 1], pg_r.at[n, r - 1], dev_x(r))

    def last_shared(n):
        for r in range(1, 8):
            gg = (g - r + 8) % 8
            rows = pl.ds(pl.multiple_of(96 * (gg % 2), 32), 96)
            arrive(grads.at[n, gg // 2, rows], direct_s.at[r - 1], direct_r.at[r - 1])

    def share(n):
        for r in range(1, 4):
            arrive(grads.at[n, (x - r + 4) % 4, mine], pg_s.at[n, r - 1], pg_r.at[n, r - 1])
        send(grads.at[n, :, mine], grads.at[n, :, mine], pgc_s.at[n], pgc_r.at[n], core)

    def shared(n):
        arrive(grads.at[n, :, theirs], pgc_s.at[n], pgc_r.at[n])

    def gradient(n):
        total = jnp.zeros((192, BLOCK), F32)
        for xx in range(4):
            total += jnp.dot(grads[n, xx], scaled[rows_of(n, xx), :], preferred_element_type=F32)
        return total

    def gain_part(n):
        total = jnp.zeros((1, BLOCK), F32)
        for xx in range(4):
            back = lax.dot_general(grads[n, xx], block, (((0,), (0,)), ((), ())), preferred_element_type=F32)
            total += jnp.sum(back * norm[rows_of(n, xx), :], axis=0, keepdims=True)
        return total

    pairs(0, near)
    pre_act(0)
    onward(3, 2)
    sum_x(0)
    onward(3, 3)
    onward(4, 0)
    onward(4, 1)
    pairs(1, side)
    pre_act(1)
    onward(4, 2)
    sum_x(1)
    pairs(2, corner, 0, 8)
    onward(4, 3)
    pairs(2, corner, 8, 16)
    pre_act(2)
    sum_x(2)
    slope(0)
    for h in range(4):
        lands(4, h)
    pairs(3, far)
    last_pre_act(3)
    last_sum_x(3)
    slope(1)
    share(0)
    shared(0)
    acc[...] = gradient(0)
    gain_sum = gain_part(0)
    slope(2)
    share(1)
    done = list(sends)
    sends.clear()
    slope(3)
    shared(1)
    acc[...] += gradient(1)
    gain_sum += gain_part(1)
    share(2)
    shared(2)
    acc[...] += gradient(2)
    gain_sum += gain_part(2)
    for one in done:
        one.wait_send()
    last_shared(3)
    rounded = (acc[...] + gradient(3)).astype(BF16)

    block_out[0] = rounded[0:96]
    block_out[1] = rounded[96:192]
    send(block_out.at[other], result.at[x, c], core_s.at[1], core_r.at[1], core)
    result[pl.ds(x, 1), pl.ds(c, 1)] = block_out[pl.ds(c, 1)][None]
    way = 1 - 2 * c

    def spread(xx, half, rows, m, k, d):
        send(result.at[xx, half, rows], result.at[xx, half, rows], res_s.at[m, k], res_r.at[m, k], dev_x(d))

    every, upper, lower = slice(0, 96), slice(0, 48), slice(48, 96)
    spread(x, c, every, c, 0, way)
    spread(x, c, upper, other, 3, -way)
    arrive(result.at[x, other], core_s.at[1], core_r.at[1])
    spread(x, other, every, other, 0, -way)
    spread(x, other, every, c, 1, way)
    spread(x, c, lower, other, 1, -way)
    gain_sum += gain_part(3)
    for k in range(6):
        gain_mine[k : k + 1, :] = gain_sum[:, k * LANES : (k + 1) * LANES]
    gain_mine[6:8, :] = jnp.zeros((2, LANES), F32)

    to_z = copy(gain_mine, gain_z.at[(apart + 7) % 8], gz_s, gz_r.at[(apart + 7) % 8], at(x, g * 16 + y * 2 + c))

    @pl.when(apart != 0)
    def _():
        to_z.start()

    def spell(xx, half):
        for k in range(6):
            col = result[xx, half, :, k * LANES : (k + 1) * LANES].astype(F32)
            out_ref[pl.ds(12 * xx + 6 * half + k, 96, stride=48), :] = col

    for half in range(2):
        spell(x, half)

    outs_y = [copy(gain_y.at[7], gain_y.at[r - 1], gy_s.at[r - 1], gy_r.at[r - 1], dev_y(r)) for r in range(1, 8)]

    @pl.when(apart == 0)
    def _():
        sum_z = gain_mine[...]
        for r in range(7):
            arrive(gain_z.at[r], gz_s, gz_r.at[r])
            sum_z += gain_z[r]
        gain_y[7] = sum_z
        for one in outs_y:
            one.start()

    behind, ahead = (x - way + 4) % 4, (x + way + 4) % 4

    def came(xx, half, rows, m, k):
        arrive(result.at[xx, half, rows], res_s.at[m, k], res_r.at[m, k])

    came(behind, c, every, c, 0)
    spread(behind, c, every, c, 2, way)
    came(ahead, other, every, other, 0)
    spread(ahead, other, every, other, 2, -way)

    outs_f = [copy(gain_out, gain_out, gf_s.at[r - 1], gf_r, mate((g + r) % 8)) for r in range(1, 8)]

    @pl.when(apart == 0)
    def _():
        sum_y = gain_y[7]
        for r in range(7):
            arrive(gain_y.at[r], gy_s.at[r], gy_r.at[r])
            sum_y += gain_y[r]
        gain_out[...] = sum_y
        for one in outs_f:
            one.start()

    spell(behind, c)
    spell(ahead, other)
    came(behind, other, every, c, 1)
    spell(behind, other)
    came(ahead, c, upper, other, 3)
    came(ahead, c, lower, other, 1)
    spell(ahead, c)

    @pl.when(apart != 0)
    def _():
        arrive(gain_out, gf_s.at[0], gf_r)
        to_z.wait_send()

    @pl.when(apart == 0)
    def _():
        for one in outs_y:
            one.wait_send()
        for one in outs_f:
            one.wait_send()

    first = 48 * (2 * y + c)
    turn = first % LANES
    line = first // LANES
    here = jnp.broadcast_to(gain_out[pl.ds(line, 1), :], (8, LANES))
    after = jnp.broadcast_to(gain_out[pl.ds(line + 1, 1), :], (8, LANES))
    back = (LANES - turn) % LANES
    moved = jnp.where(lane_iota(8) < LANES - turn, pltpu.roll(here, back, 1), pltpu.roll(after, back, 1))
    out_ref[4608:4616, :] = moved

    arrive(result.at[(x + 2) % 4, 0], res_s.at[0, 2], res_r.at[0, 2])
    spell((x + 2) % 4, 0)
    arrive(result.at[(x + 2) % 4, 1], res_s.at[1, 2], res_r.at[1, 2])
    spell((x + 2) % 4, 1)
    for one in sends:
        one.wait_send()


def body(tokens, act_cot, old_slots, offsets):
    vmem = pl.BlockSpec(memory_space=pltpu.VMEM)
    smem = pl.BlockSpec(memory_space=pltpu.SMEM)
    dma = pltpu.SemaphoreType.DMA
    slots = jnp.pad(old_slots, (0, LINES * LANES - old_slots.shape[0])).reshape(LINES, LANES)
    chips = chips_in_order()
    away = np.array([[AWAY[chip[axis]] for chip in chips for _ in range(8)] for axis in range(2)], np.int32)
    n = np.arange(BLOCK)
    lanes = np.arange(LANES)[:, None]
    pick = jnp.asarray((lanes == 16 + n % 48).astype(np.float32), BF16)
    mask = jnp.asarray((np.arange(16)[:, None] == n // 48).astype(np.float32))
    out = pl.pallas_call(
        main_kernel,
        out_shape=jax.ShapeDtypeStruct((4616, LANES), F32),
        in_specs=[vmem, vmem, smem, vmem, vmem, vmem, vmem],
        out_specs=vmem,
        scratch_shapes=[
            pltpu.VMEM((FRONT + LINES + BACK, LANES), F32),
            pltpu.VMEM((96 * 16, LANES), F32),
            pltpu.VMEM((256, LANES), F32),
            pltpu.VMEM((8, 32, LANES), BF16),
            pltpu.VMEM((8, 32, LANES), BF16),
            pltpu.VMEM((2, 96, BLOCK), BF16),
            pltpu.VMEM((2, 32, BLOCK), BF16),
            pltpu.VMEM((2, 32, BLOCK), BF16),
            pltpu.VMEM((2, 32, BLOCK), BF16),
            pltpu.VMEM((2, 32, BLOCK), BF16),
            pltpu.VMEM((2, 96, BLOCK), BF16),
            pltpu.VMEM((2, 96, BLOCK), BF16),
            pltpu.VMEM((2, 8, LANES), F32),
            pltpu.VMEM((8, 8, A_ROWS, LANES), BF16),
            pltpu.VMEM((8, 8, B_ROWS, LANES), BF16),
            pltpu.VMEM((96, 512), F32),
            pltpu.VMEM((2048, BLOCK), F32),
            pltpu.VMEM((2048, BLOCK), BF16),
            pltpu.VMEM((SETS, 2, 4, 96, SIZE), F32),
            pltpu.VMEM((SETS, 4, 96, SIZE), F32),
            pltpu.VMEM((SETS, 4, 96, SIZE), F32),
            pltpu.VMEM((SETS, 3, 96, SIZE), F32),
            pltpu.VMEM((SETS, 4, 192, SIZE), BF16),
            pltpu.VMEM((192, BLOCK), F32),
            pltpu.VMEM((4, 2, 96, BLOCK), BF16),
            pltpu.VMEM((2, 96, BLOCK), BF16),
            pltpu.VMEM((8, LANES), F32),
            pltpu.VMEM((8, LANES), F32),
            pltpu.VMEM((8, LANES), F32),
            pltpu.VMEM((8, 8, LANES), F32),
            pltpu.VMEM((16, LANES), F32),
            pltpu.VMEM((8, LANES), F32),
            pltpu.VMEM((8, 8, LANES), F32),
            pltpu.VMEM((8, 8, LANES), F32),
            pltpu.VMEM((8, LANES), F32),
            dma((7,)), dma((7,)),
            dma((2,)), dma((2,)),
            dma((4,)), dma((4,)),
            dma((2, 7)), dma((2, 7)),
            dma((4, 4, 4)), dma((4, 4, 4)),
            dma((SETS,)), dma((SETS,)),
            dma((SETS, 3)), dma((SETS, 3)),
            dma((SETS, 3)), dma((SETS, 3)),
            dma((SETS,)), dma((SETS,)),
            dma((4,)), dma((4,)),
            dma((7,)), dma((7,)),
            dma((2, 4)), dma((2, 4)),
            dma((7,)), dma((7,)),
            dma((7,)), dma,
            dma, dma((8,)),
            dma((7,)), dma((7,)),
            dma((7,)), dma,
        ],
        compiler_params=pltpu.CompilerParams(
            collective_id=0, has_side_effects=True, vmem_limit_bytes=40 * 2**20
        ),
    )(tokens, slots, offsets, act_cot[0].T, jnp.asarray(away), pick, mask)
    return out.reshape(-1)[:SHARD]


def solution(mesh):
    placed = (P("dp", "fsdp", None), P("dp", None, "fsdp"), P("fsdp"), P())
    return jax.shard_map(body, mesh=mesh, in_specs=placed, out_specs=P("fsdp"), check_vma=False)
```
